32 devices in a mesh: query: 4 (over y, x), corpus: 8 (over z, core).
Axes of the slice: x: 2, y: 2, z: 4, core: 2. Of those that a mesh axis runs over, the one named last changes fastest.
Arguments:
- queries: float32 [1536, 768], P('query'), may hold values from -20 to 20
- codes: int32 [8192, 96], P('corpus'), may hold values from 0 to 255
- positive: int32 [1536], P('query'), may hold values from 0 to 8191
- codebook: float32 [256, 768], replicated, may hold values from -0.6 to 0.6
Outputs:
- grad_queries: float32 [1536, 768], P('query')
- grad_codebook: float32 [256, 768], replicated
- loss: float32 [1536], P('query')
The draws below stay inside these ranges and needn't reach their ends.
All inputs are finite; a program needn't handle non-finite values.
Results may differ from the reference program's by a relative error of at most 0.0003.
Values sent between devices are 32-bit elements; how exact they have to be, the bound alone decides.
No kernel may reach another device: no remote copies, remote signals or barrier semaphores. Data moves between devices by JAX's collectives and lax.ppermute only.
A program may use at most 64 MiB of HBM per device.

```python
import math
import jax
import jax.numpy as jnp
from jax import lax

D = 768
SUB = 96
CW = 256
DOC_DEV = 1024
NQ = 1536
ND = 8192
N_CORPUS = 8


def make_codes(key):
    base = jax.random.randint(jax.random.fold_in(key, 11), (ND, SUB), 0, CW, dtype=jnp.int32)
    offset = jax.random.randint(jax.random.fold_in(key, 12), (ND, SUB), 1, CW, dtype=jnp.int32)
    row_ids = jnp.arange(ND, dtype=jnp.int32)[:, None]
    sub_ids = jnp.arange(SUB, dtype=jnp.int32)[None, :]
    before = jnp.concatenate([base[:1], base[:-1]], axis=0)
    changed = sub_ids == row_ids // 64 % SUB
    twin_codes = jnp.where(changed, (before + offset) % CW, before)
    return jnp.where(row_ids % 64 == 1, twin_codes, base)


def make_positive(key):
    drawn = jax.random.randint(jax.random.fold_in(key, 31), (NQ,), 0, ND, dtype=jnp.int32)
    return drawn.at[NQ - 1].set(ND - 1)


def make_codebook(key):
    factor = 3.0 / math.sqrt(D)
    values = jnp.clip(jax.random.normal(jax.random.fold_in(key, 21), (CW, D), jnp.float32), -5.0, 5.0)
    return jnp.clip(values * factor, -0.6, 0.6)


def draw_codes(key, part):
    return make_codes(key)


def draw_positive(key, part):
    return make_positive(key)


def draw_codebook(key, part):
    return make_codebook(key)


def draw_queries(key, part):
    noise = jnp.clip(jax.random.normal(jax.random.fold_in(key, 41), (NQ, D), jnp.float32), -5.0, 5.0)
    return noise


def setup_inputs(seed: int = 0) -> dict:
    arg_keys = jax.random.split(jax.random.key(seed), 5)
    queries = draw_queries(jax.random.fold_in(arg_keys[4], 71), 0)
    codes = draw_codes(jax.random.fold_in(arg_keys[4], 71), 0)
    positive = draw_positive(jax.random.fold_in(arg_keys[4], 71), 0)
    codebook = draw_codebook(jax.random.fold_in(arg_keys[4], 71), 0)
    return dict(queries=queries, codes=codes, positive=positive, codebook=codebook)


precise = lax.Precision.HIGHEST


def rebuild(codebook, codes_block):
    columns = jnp.repeat(codes_block, D // SUB, axis=1)
    return jnp.take_along_axis(codebook, columns, axis=0), columns


def reference(queries, codes, positive, codebook):
    codes_blocks = codes.reshape(N_CORPUS, DOC_DEV, SUB)

    def stats_step(carry, codes_block):
        row_top, row_total = carry
        rebuilt, unused = rebuild(codebook, codes_block)
        scores = lax.dot_general(queries, rebuilt, (((1,), (1,)), ((), ())), precision=precise, preferred_element_type=jnp.float32)
        new_top = jnp.maximum(row_top, jnp.max(scores, axis=1))
        new_total = row_total * jnp.exp(row_top - new_top) + jnp.sum(jnp.exp(scores - new_top[:, None]), axis=1)
        return (new_top, new_total), None

    start_top = jnp.full((NQ,), -jnp.inf, dtype=jnp.float32)
    start_total = jnp.zeros((NQ,), dtype=jnp.float32)
    (row_top, row_total), unused = lax.scan(stats_step, (start_top, start_total), codes_blocks)
    pos_docs, unused = rebuild(codebook, codes[positive])
    pos_score = jnp.sum(queries * pos_docs, axis=1)
    log_total = row_top + jnp.log(row_total)
    loss = log_total - pos_score
    column_ids = jnp.arange(D, dtype=jnp.int32)[None, :]

    def grad_step(carry, inputs):
        query_grad, codebook_grad = carry
        block_index, codes_block = inputs
        rebuilt, columns = rebuild(codebook, codes_block)
        scores = lax.dot_general(queries, rebuilt, (((1,), (1,)), ((), ())), precision=precise, preferred_element_type=jnp.float32)
        doc_ids = block_index * DOC_DEV + jnp.arange(DOC_DEV, dtype=jnp.int32)
        positive_hits = (positive[:, None] == doc_ids[None, :]).astype(jnp.float32)
        weights = jnp.exp(scores - log_total[:, None]) - positive_hits
        query_grad = query_grad + jnp.dot(weights, rebuilt, precision=precise, preferred_element_type=jnp.float32)
        doc_grad = lax.dot_general(weights, queries, (((0,), (0,)), ((), ())), precision=precise, preferred_element_type=jnp.float32)
        codebook_grad = codebook_grad.at[columns, column_ids].add(doc_grad)
        return (query_grad, codebook_grad), None

    start = (jnp.zeros((NQ, D), dtype=jnp.float32), jnp.zeros((CW, D), dtype=jnp.float32))
    block_ids = jnp.arange(N_CORPUS, dtype=jnp.int32)
    (grad_queries, grad_codebook), unused = lax.scan(grad_step, start, (block_ids, codes_blocks))
    return (grad_queries, grad_codebook, loss)
```

```python
import functools

import jax
import jax.numpy as jnp
from jax import lax
from jax.experimental import pallas as pl
from jax.experimental.pallas import tpu as pltpu
from jax.sharding import PartitionSpec as P

F32, BF16, I32 = jnp.float32, jnp.bfloat16, jnp.int32
LANES = 128


def split2(x):
    high = x.astype(BF16)
    return high, (x - high.astype(F32)).astype(BF16)


def split3(x):
    high = x.astype(BF16)
    rest = x - high.astype(F32)
    mid = rest.astype(BF16)
    return high, mid, (rest - mid.astype(F32)).astype(BF16)


def dot(a, b):
    return jnp.dot(a, b, preferred_element_type=F32)


def dot_nt(a, b):
    return lax.dot_general(a, b, (((1,), (1,)), ((), ())), preferred_element_type=F32)


def score_kernel(q_ref, codes_t_ref, book_t_ref, pos_ref, e_ref, r_ref, stats_ref, qs_ref, s_ref, low_ref):
    rows, width = q_ref.shape
    subs, docs = codes_t_ref.shape
    words = book_t_ref.shape[1]
    sub_width = width // subs
    high, mid, low = split3(q_ref[...])
    qs_ref[:, 0:width] = low
    qs_ref[:, width : 2 * width] = mid
    qs_ref[:, 2 * width : 3 * width] = high

    def rebuild(g, _):
        first = pl.multiple_of(g * 8, 8)
        block = codes_t_ref[pl.ds(first, 8), :]
        for pair in range(4):
            out_row = pl.multiple_of(g * 8 * sub_width + pair * 16, 16)
            tables = [book_t_ref[pl.ds(out_row + 8 * k, 8), :] for k in range(2)]
            for d in range(docs // LANES):
                lanes = slice(d * LANES, (d + 1) * LANES)
                halves = []
                for k in range(2):
                    code = jnp.broadcast_to(block[2 * pair + k : 2 * pair + k + 1, lanes], (8, LANES))
                    inner = code & (LANES - 1)
                    value = jnp.take_along_axis(tables[k][:, :LANES], inner, axis=1)
                    for w in range(1, words // LANES):
                        other = jnp.take_along_axis(tables[k][:, w * LANES : (w + 1) * LANES], inner, axis=1)
                        value = jnp.where(code >= w * LANES, other, value)
                    halves.append(value)
                high, mid, low = split3(jnp.concatenate(halves, axis=0))
                r_ref[pl.ds(out_row, 16), lanes] = high
                r_ref[pl.ds(out_row + width, 16), lanes] = mid
                low_ref[pl.ds(out_row, 16), lanes] = low
        return 0

    lax.fori_loop(0, subs // 8, rebuild, 0)

    tile = 256

    def score(t, _):
        lanes = pl.ds(pl.multiple_of(t * tile, tile), tile)
        small = dot(qs_ref[:, 0 : 2 * width], r_ref[:, lanes]) + dot(qs_ref[:, 2 * width :], low_ref[:, lanes])
        middle = dot(qs_ref[:, width:], r_ref[:, lanes])
        s_ref[:, lanes] = (small + middle) + dot(qs_ref[:, 2 * width :], r_ref[0:width, lanes])
        return 0

    lax.fori_loop(0, docs // tile, score, 0)
    s = s_ref[...]
    top = jnp.max(s, axis=1, keepdims=True)
    e = jnp.exp(s - top)
    e_ref[...] = e
    total = jnp.sum(e, axis=1, keepdims=True)
    hits = pos_ref[...] == lax.broadcasted_iota(I32, s.shape, 1)
    own = jnp.sum(jnp.where(hits, s, 0.0), axis=1, keepdims=True)
    lane = lax.broadcasted_iota(I32, (rows, LANES), 1)
    packed = jnp.where(lane == 0, top, jnp.where(lane == 1, total, jnp.where(lane == 2, own, 0.0)))
    stats_ref[...] = packed.T[0:8, :]


def query_kernel(e_ref, pos_ref, r_ref, u_ref, p_ref):
    rows, docs = e_ref.shape
    width = u_ref.shape[1]
    eh, em = split2(e_ref[...])
    hits = (pos_ref[...] == lax.broadcasted_iota(I32, (rows, docs), 1)).astype(F32).astype(BF16)
    tile = 256

    def step(t, _):
        first = pl.multiple_of(t * tile, tile)
        rh = r_ref[pl.ds(first, tile), :]
        rm = r_ref[pl.ds(first + width, tile), :]
        u_ref[:, pl.ds(first, tile)] = (dot_nt(em, rh) + dot_nt(eh, rm)) + dot_nt(eh, rh)
        p_ref[:, pl.ds(first, tile)] = dot_nt(hits, rm) + dot_nt(hits, rh)
        return 0

    lax.fori_loop(0, width // tile, step, 0)


def book_kernel(e_ref, pos_ref, scale_ref, q_ref, codes_t_ref, out_ref, ws_ref, qt_ref, dg_ref, gt_ref):
    rows, docs = e_ref.shape
    width = q_ref.shape[1]
    subs = codes_t_ref.shape[0]
    sub_width = width // subs
    words = out_ref.shape[0]
    hits = pos_ref[...] == lax.broadcasted_iota(I32, (rows, docs), 1)
    w = e_ref[...] * scale_ref[...] - jnp.where(hits, 1.0, 0.0)
    wh, wm = split2(w)
    ws_ref[0:rows, :] = wh
    ws_ref[rows : 2 * rows, :] = wm
    qh, qm = split2(q_ref[...].T)
    qt_ref[:, 0:rows] = qm
    qt_ref[:, rows : 2 * rows] = qh
    tile = 256

    def grad(t, _):
        lanes = pl.ds(pl.multiple_of(t * tile, tile), tile)
        dg_ref[:, lanes] = dot(qt_ref[...], ws_ref[:, lanes]) + dot(qt_ref[:, rows:], ws_ref[0:rows, lanes])
        return 0

    lax.fori_loop(0, docs // tile, grad, 0)

    fine = 64
    coarse = words // fine

    def scatter(g, _):
        first = pl.multiple_of(g * 8, 8)
        block = codes_t_ref[pl.ds(first, 8), :]
        for half in range(2):
            lhs, rhs = [], []
            for s in range(4):
                sub = half * 4 + s
                code = block[sub : sub + 1, :]
                row = pl.multiple_of(g * 8 * sub_width + sub * 8, 8)
                value = dg_ref[pl.ds(row, 8), :]
                high = value.astype(BF16).astype(F32)
                rest = value - high
                outer = jnp.broadcast_to(code // fine, value.shape)
                for piece in (high, rest):
                    for b in range(coarse):
                        lhs.append(jnp.where(outer == b, piece, 0.0))
                inner = jnp.broadcast_to(code & (fine - 1), (fine, docs))
                rhs.append(jnp.where(inner == lax.broadcasted_iota(I32, (fine, docs), 0), 1.0, 0.0))
            lhs = jnp.concatenate(lhs, axis=0).astype(BF16)
            rhs = jnp.concatenate(rhs, axis=0).astype(BF16)
            out = dot_nt(lhs, rhs)
            span = coarse * 8
            for s in range(4):
                both = out[2 * span * s : 2 * span * s + span, :] + out[2 * span * s + span : 2 * span * (s + 1), :]
                mine = both[:, s * fine : (s + 1) * fine]
                parts = [mine[8 * b : 8 * b + 8, :] for b in range(coarse)]
                row = pl.multiple_of(g * 8 * sub_width + (half * 4 + s) * 8, 8)
                gt_ref[pl.ds(row, 8), :] = jnp.concatenate(parts, axis=1)
        return 0

    lax.fori_loop(0, subs // 8, scatter, 0)
    out_ref[...] = gt_ref[...].T


def pairs(axis, bits):
    return [(i, i ^ bits) for i in range(lax.axis_size(axis))]


def swap(x, axis, bits):
    return lax.ppermute(x, axis, pairs(axis, bits))


def pick(parts, index):
    return lax.dynamic_index_in_dim(parts, index, 0, keepdims=False)


def scatter_sum(x, axis, place, count, unit):
    parts = x.reshape((count, x.shape[0] // count) + x.shape[1:])
    got = [swap(pick(parts, place ^ k), axis, k * unit) for k in range(1, count)]
    mine = pick(parts, place)
    for piece in got:
        mine = mine + piece
    return mine


def gather(x, axis, place, count, unit):
    got = [x] + [swap(x, axis, k * unit) for k in range(1, count)]
    out = jnp.zeros((count,) + x.shape, x.dtype)
    for k, piece in enumerate(got):
        out = lax.dynamic_update_index_in_dim(out, piece, place ^ k, 0)
    return out.reshape((count * x.shape[0],) + x.shape[1:])


def join_stats(a, b):
    top = jnp.maximum(a[0], b[0])
    total = a[1] * jnp.exp(a[0] - top) + b[1] * jnp.exp(b[0] - top)
    return jnp.stack([top, total, a[2] + b[2]])


VMEM = pl.BlockSpec(memory_space=pltpu.VMEM)


def local(queries, codes, positive, codebook):
    rows, width = queries.shape
    docs, subs = codes.shape
    words = codebook.shape[0]
    codes_t = codes.T
    book_t = codebook.T
    rel = (positive - lax.axis_index("corpus") * docs)[:, None]
    e, r, stats = pl.pallas_call(
        score_kernel,
        out_shape=(
            jax.ShapeDtypeStruct((rows, docs), F32),
            jax.ShapeDtypeStruct((2 * width, docs), BF16),
            jax.ShapeDtypeStruct((8, rows), F32),
        ),
        in_specs=[VMEM] * 4,
        out_specs=[VMEM] * 3,
        scratch_shapes=[pltpu.VMEM((rows, 3 * width), BF16), pltpu.VMEM((rows, docs), F32), pltpu.VMEM((width, docs), BF16)],
        compiler_params=pltpu.CompilerParams(vmem_limit_bytes=32 * 2**20),
        name="scores",
    )(queries, codes_t, book_t, rel)
    corpus, query = lax.axis_size("corpus"), lax.axis_size("query")
    me = lax.axis_index("corpus")
    core, chip, chips = me % 2, me // 2, corpus // 2
    plane = lax.axis_index("query")
    top = stats[0]
    joined = stats[0:3]
    bits = 1
    while bits < corpus:
        joined = join_stats(joined, swap(joined, "corpus", bits))
        bits *= 2
    log_total = joined[0] + jnp.log(joined[1])
    loss = log_total - joined[2]
    scale = jnp.exp(top - log_total)[:, None]
    u, p = pl.pallas_call(
        query_kernel,
        out_shape=(jax.ShapeDtypeStruct((rows, width), F32), jax.ShapeDtypeStruct((rows, width), F32)),
        in_specs=[VMEM] * 3,
        out_specs=[VMEM] * 2,
        compiler_params=pltpu.CompilerParams(vmem_limit_bytes=32 * 2**20),
        name="query_terms",
    )(e, rel, r)
    terms = u * scale - p
    book = pl.pallas_call(
        book_kernel,
        out_shape=jax.ShapeDtypeStruct((words, width), F32),
        in_specs=[VMEM] * 5,
        out_specs=VMEM,
        scratch_shapes=[
            pltpu.VMEM((2 * rows, docs), BF16),
            pltpu.VMEM((width, 2 * rows), BF16),
            pltpu.VMEM((width, docs), F32),
            pltpu.VMEM((width, words), F32),
        ],
        compiler_params=pltpu.CompilerParams(vmem_limit_bytes=32 * 2**20),
        name="book_terms",
    )(e, rel, scale, queries, codes_t)
    part = scatter_sum(terms, "corpus", core, 2, 1)
    part = scatter_sum(part, "corpus", chip, chips, 2)
    part = gather(part, "corpus", chip, chips, 2)
    grad_queries = gather(part, "corpus", core, 2, 1)
    part = scatter_sum(book, "corpus", core, 2, 1)
    part = scatter_sum(part, "query", plane, query, 1)
    part = scatter_sum(part, "corpus", chip, chips, 2)
    part = gather(part, "corpus", chip, chips, 2)
    part = gather(part, "query", plane, query, 1)
    grad_codebook = gather(part, "corpus", core, 2, 1)
    return grad_queries, grad_codebook, loss


def solution(mesh):
    placed = (P("query", None), P("corpus", None), P("query"), P())
    return jax.shard_map(
        local,
        mesh=mesh,
        in_specs=placed,
        out_specs=(P("query", None), P(), P("query")),
        check_vma=False,
    )
```

```python
import jax
import jax.numpy as jnp
from jax import lax
from jax.experimental import pallas as pl
from jax.experimental.pallas import tpu as pltpu
from jax.sharding import PartitionSpec as P

F32, BF16, I32 = jnp.float32, jnp.bfloat16, jnp.int32
LANES = 128
FINE = 64
VMEM = pl.BlockSpec(memory_space=pltpu.VMEM)
ANY = pl.BlockSpec(memory_space=pl.ANY)


def split2(x):
    high = x.astype(BF16)
    return high, (x - high.astype(F32)).astype(BF16)


def split3(x):
    high = x.astype(BF16)
    rest = x - high.astype(F32)
    mid = rest.astype(BF16)
    return high, mid, (rest - mid.astype(F32)).astype(BF16)


def dot(a, b):
    return jnp.dot(a, b, preferred_element_type=F32)


def dot_nt(a, b):
    return lax.dot_general(a, b, (((1,), (1,)), ((), ())), preferred_element_type=F32)


def column(row):
    return jnp.broadcast_to(row, (LANES, row.shape[1])).T


def pick_lanes(table, code):
    inner = code & (LANES - 1)
    value = None
    for w in range(table.shape[1] // LANES):
        part = jnp.take_along_axis(
            table[:, w * LANES : (w + 1) * LANES], inner, axis=1, mode="promise_in_bounds"
        )
        value = part if w == 0 else jnp.where(code >= w * LANES, part, value)
    return value


def score_kernel(
    q_hbm, codes_hbm, book_hbm, pos_hbm,
    e_ref, hits_ref, r_ref, stats_ref,
    q_ref, codes_ref, book_ref, pos_ref, qs_ref, s_ref, low_ref, book_t_ref, sems,
):
    rows, width = q_ref.shape
    subs, docs = codes_ref.shape
    loads = [
        pltpu.make_async_copy(src, dst, sems.at[i])
        for i, (src, dst) in enumerate(
            [(book_hbm, book_ref), (codes_hbm, codes_ref), (q_hbm, q_ref), (pos_hbm, pos_ref)]
        )
    ]
    for load in loads:
        load.start()
    loads[0].wait()
    book_t_ref[...] = book_ref[...].T
    loads[1].wait()
    loads[2].wait()
    loads[3].wait()
    high, mid, low = split3(q_ref[...])
    qs_ref[:, 0:width] = low
    qs_ref[:, width : 2 * width] = mid
    qs_ref[:, 2 * width : 3 * width] = high
    tile = 256
    for t in range(docs // tile):
        for sub in range(0, subs, 2):
            for d in range(t * tile, (t + 1) * tile, LANES):
                lanes = slice(d, d + LANES)
                halves = [
                    pick_lanes(
                        book_t_ref[8 * s : 8 * s + 8, :],
                        jnp.broadcast_to(codes_ref[s : s + 1, lanes], (8, LANES)),
                    )
                    for s in (sub, sub + 1)
                ]
                high, mid, low = split3(jnp.concatenate(halves, axis=0))
                r_ref[8 * sub : 8 * sub + 16, lanes] = high
                r_ref[width + 8 * sub : width + 8 * sub + 16, lanes] = mid
                low_ref[8 * sub : 8 * sub + 16, lanes] = low
        lanes = slice(t * tile, (t + 1) * tile)
        small = dot(qs_ref[:, 0 : 2 * width], r_ref[:, lanes]) + dot(
            qs_ref[:, 2 * width :], low_ref[:, lanes]
        )
        middle = dot(qs_ref[:, width:], r_ref[:, lanes])
        s_ref[:, lanes] = (small + middle) + dot(qs_ref[:, 2 * width :], r_ref[0:width, lanes])
    s = s_ref[...]
    top = jnp.max(s, axis=1, keepdims=True)
    e = jnp.exp(s - top)
    e_ref[...] = e
    total = jnp.sum(e, axis=1, keepdims=True)
    wanted = column(pos_ref[...].reshape(1, rows) - lax.axis_index("corpus") * docs)[:, 0:1]
    hits = wanted == lax.broadcasted_iota(I32, s.shape, 1)
    hits_ref[...] = jnp.where(hits, 1.0, 0.0).astype(BF16)
    own = jnp.sum(jnp.where(hits, s, 0.0), axis=1, keepdims=True)
    lane = lax.broadcasted_iota(I32, (rows, LANES), 1)
    packed = jnp.where(lane == 0, top, jnp.where(lane == 1, total, jnp.where(lane == 2, own, 0.0)))
    stats_ref[...] = packed.T[0:8, :]


def spread_kernel(e_ref, r_ref, u_ref):
    width = u_ref.shape[1]
    eh, em = split2(e_ref[...])
    rh, rm = r_ref[0:width, :], r_ref[width:, :]
    u_ref[...] = (dot_nt(em, rh) + dot_nt(eh, rm)) + dot_nt(eh, rh)


def positive_kernel(hits_ref, r_ref, q_hbm, after_ref, p_ref, qt_ref, q_ref, sem):
    rows, width = p_ref.shape
    load = pltpu.make_async_copy(q_hbm, q_ref, sem)
    load.start()
    hits = hits_ref[...]
    p_ref[...] = dot_nt(hits, r_ref[width:, :]) + dot_nt(hits, r_ref[0:width, :])
    load.wait()
    high, mid = split2(q_ref[...].T)
    qt_ref[:, 0:rows] = mid
    qt_ref[:, rows : 2 * rows] = high


def join(a, b):
    top = jnp.maximum(a[0:1], b[0:1])
    total = a[1:2] * jnp.exp(a[0:1] - top) + b[1:2] * jnp.exp(b[0:1] - top)
    return top, total, a[2:3] + b[2:3]


def join_kernel(a_ref, b_ref, after_ref, out_ref):
    top, total, own = join(a_ref[...], b_ref[...])
    out_ref[0:1, :] = top
    out_ref[1:2, :] = total
    out_ref[2:3, :] = own


def terms_kernel(a_ref, b_ref, first_ref, u_ref, p_ref, keep_ref, send_ref, loss_ref, scale_ref, scale_col):
    top, total, own = join(a_ref[...], b_ref[...])
    log_total = top + jnp.log(total)
    loss_ref[...] = (log_total - own).reshape(loss_ref.shape)
    scale = jnp.exp(first_ref[0:1, :] - log_total)
    scale_ref[...] = scale
    half = keep_ref.shape[0]
    scale_col[...] = column(scale).reshape(2, half, LANES)
    core = lax.axis_index("corpus") % 2
    keep_ref[...] = u_ref[core] * scale_col[core][:, 0:1] - p_ref[core]
    send_ref[...] = u_ref[1 - core] * scale_col[1 - core][:, 0:1] - p_ref[1 - core]


def book_kernel(
    e_ref, hits_ref, scale_ref, qt_ref, codes_ref, after_ref,
    keep_ref, send_ref, ws_ref, dg_ref, gt_ref, both_ref,
):
    rows, docs = e_ref.shape
    width, words = gt_ref.shape
    subs = codes_ref.shape[0]
    w = e_ref[...] * column(scale_ref[...])[:, 0:1] - hits_ref[...].astype(F32)
    wh, wm = split2(w)
    ws_ref[0:rows, :] = wh
    ws_ref[rows:, :] = wm
    dg_ref[...] = dot(qt_ref[...], ws_ref[...]) + dot(qt_ref[:, rows:], ws_ref[0:rows, :])
    coarse = words // FINE
    ramp = lax.broadcasted_iota(I32, (FINE, docs), 0).astype(F32).astype(BF16)
    for first in range(0, subs, 4):
        lhs, rhs = [], []
        for sub in range(first, first + 4):
            code = codes_ref[sub : sub + 1, :]
            value = dg_ref[8 * sub : 8 * sub + 8, :]
            high = value.astype(BF16).astype(F32)
            both = jnp.concatenate([high, value - high], axis=0).astype(BF16)
            outer = jnp.broadcast_to((code // FINE).astype(F32), (16, docs)).astype(BF16)
            lhs += [jnp.where(outer == jnp.bfloat16(b), both, jnp.zeros_like(both)) for b in range(coarse)]
            inner = jnp.broadcast_to((code & (FINE - 1)).astype(F32), (16, docs)).astype(BF16)
            inner = jnp.concatenate([inner] * (FINE // 16), axis=0)
            rhs.append(jnp.where(inner == ramp, jnp.ones_like(ramp), jnp.zeros_like(ramp)))
        out = dot_nt(jnp.concatenate(lhs, axis=0), jnp.concatenate(rhs, axis=0))
        for s in range(4):
            mine = out[16 * coarse * s : 16 * coarse * (s + 1), s * FINE : (s + 1) * FINE]
            parts = [mine[16 * b : 16 * b + 8, :] + mine[16 * b + 8 : 16 * b + 16, :] for b in range(coarse)]
            sub = first + s
            gt_ref[8 * sub : 8 * sub + 8, :] = jnp.concatenate(parts, axis=1)
    both_ref[...] = gt_ref[...].T.reshape(both_ref.shape)
    core = lax.axis_index("corpus") % 2
    keep_ref[...] = both_ref[core]
    send_ref[...] = both_ref[1 - core]


def call(kernel, outs, ins, scratch=(), flops=0, mib=16, name=None):
    return pl.pallas_call(
        kernel,
        out_shape=tuple(jax.ShapeDtypeStruct(shape, kind) for shape, kind in outs),
        in_specs=ins,
        out_specs=tuple(VMEM for _ in outs),
        scratch_shapes=list(scratch),
        compiler_params=pltpu.CompilerParams(vmem_limit_bytes=mib * 2**20),
        cost_estimate=pl.CostEstimate(flops=flops, bytes_accessed=2**17, transcendentals=0),
        name=name or kernel.__name__,
    )


def swap(x, axis, bits):
    return lax.ppermute(x, axis, [(i, i ^ bits) for i in range(lax.axis_size(axis))])


def place_of(axis, unit):
    return lax.axis_index(axis) // unit


def cut(keep, got, axis, unit, count, after, name):
    rows, width = keep.shape
    shape = (count, rows // count, width)

    def kernel(keep_ref, got_ref, after_ref, *outs):
        place = place_of(axis, unit)
        for k, out in enumerate(outs):
            out[...] = keep_ref[place ^ k] + got_ref[place ^ k]

    blocks = call(kernel, [(shape[1:], F32)] * count, [VMEM, VMEM, ANY], mib=4, name=name)(
        keep.reshape(shape), got.reshape(shape), after
    )
    return list(blocks)


def add(pieces, after, name):
    def kernel(*refs):
        total = refs[0][...]
        for ref in refs[1:-2]:
            total = total + ref[...]
        refs[-1][...] = total

    return call(kernel, [(pieces[0].shape, F32)], [VMEM] * len(pieces) + [ANY], mib=4, name=name)(*pieces, after)[0]


def put(pieces, axis, unit, name):
    rows, width = pieces[0].shape

    def kernel(*refs):
        place = place_of(axis, unit)
        for k, ref in enumerate(refs[:-1]):
            refs[-1][place ^ k] = ref[...]

    count = len(pieces)
    whole = call(kernel, [((count, rows, width), F32)], [VMEM] * count, mib=4, name=name)(*pieces)[0]
    return whole.reshape(count * rows, width)


def finish(own, got, name):
    rows, width = own.shape

    def kernel(own_ref, got_ref, out_hbm, sems):
        core = lax.axis_index("corpus") % 2
        copies = [
            pltpu.make_async_copy(own_ref, out_hbm.at[core], sems.at[0]),
            pltpu.make_async_copy(got_ref, out_hbm.at[1 - core], sems.at[1]),
        ]
        for copy in copies:
            copy.start()
        for copy in copies:
            copy.wait()

    whole = pl.pallas_call(
        kernel,
        out_shape=jax.ShapeDtypeStruct((2, rows, width), F32),
        in_specs=[VMEM, VMEM],
        out_specs=ANY,
        scratch_shapes=[pltpu.SemaphoreType.DMA((2,))],
        compiler_params=pltpu.CompilerParams(vmem_limit_bytes=4 * 2**20),
        name=name,
    )(own, got)
    return whole.reshape(2 * rows, width)


def local(queries, codes, positive, codebook):
    rows, width = queries.shape
    docs, subs = codes.shape
    words = codebook.shape[0]
    corpus, query = lax.axis_size("corpus"), lax.axis_size("query")
    chips = corpus // 2
    codes_t = codes.T
    work = rows * docs * width
    e, hits, r, stats = call(
        score_kernel,
        [((rows, docs), F32), ((rows, docs), BF16), ((2 * width, docs), BF16), ((8, rows), F32)],
        [ANY] * 4,
        [
            pltpu.VMEM((rows, width), F32),
            pltpu.VMEM((subs, docs), I32),
            pltpu.VMEM((words, width), F32),
            pltpu.VMEM((rows,), I32),
            pltpu.VMEM((rows, 3 * width), BF16),
            pltpu.VMEM((rows, docs), F32),
            pltpu.VMEM((width, docs), BF16),
            pltpu.VMEM((width, words), F32),
            pltpu.SemaphoreType.DMA((4,)),
        ],
        12 * work,
        24,
    )(queries, codes_t, codebook, positive)
    u = call(spread_kernel, [((rows, width), F32)], [VMEM] * 2, (), 6 * work)(e, r)[0]
    joined, got, bits, after = stats, swap(stats, "corpus", 1), 2, stats
    while bits < corpus:
        joined = call(join_kernel, [((8, rows), F32)], [VMEM] * 3, mib=4)(joined, got, after)[0]
        got = swap(joined, "corpus", bits)
        after = u
        bits *= 2
    p, qt = call(
        positive_kernel,
        [((rows, width), F32), ((width, 2 * rows), BF16)],
        [VMEM, VMEM, ANY, VMEM],
        [pltpu.VMEM((rows, width), F32), pltpu.SemaphoreType.DMA],
        4 * work,
    )(hits, r, queries, joined)
    half = rows // 2
    keep, send, loss, scale = call(
        terms_kernel,
        [((half, width), F32), ((half, width), F32), ((rows,), F32), ((1, rows), F32)],
        [VMEM] * 5,
        [pltpu.VMEM((2, half, LANES), F32)],
        mib=8,
    )(joined, got, stats, u.reshape(2, half, width), p.reshape(2, half, width))

    cuts = cut(keep, swap(send, "corpus", 1), "corpus", 2, chips, scale, "query_cut")
    got = [swap(cuts[k], "corpus", 2 * k) for k in range(1, chips)]

    part_rows = words // 2
    book_keep, book_send = call(
        book_kernel,
        [((part_rows, width), F32)] * 2,
        [VMEM] * 6,
        [
            pltpu.VMEM((2 * rows, docs), BF16),
            pltpu.VMEM((width, docs), F32),
            pltpu.VMEM((width, words), F32),
            pltpu.VMEM((2, part_rows, width), F32),
        ],
        14 * work,
    )(e, hits, scale, qt, codes_t, cuts[0])

    own = add([cuts[0]] + got, scale, "query_sum")
    blocks = [own] + [swap(own, "corpus", 2 * k) for k in range(1, chips)]
    whole = put(blocks, "corpus", 2, "query_put")
    grad_queries = finish(whole, swap(whole, "corpus", 1), "query_finish")

    cuts = cut(book_keep, swap(book_send, "corpus", 1), "query", 1, query, scale, "book_cut")
    got = [swap(cuts[k], "query", k) for k in range(1, query)]
    own = add([cuts[0]] + got, scale, "book_sum")
    bits = 2
    while bits < corpus:
        own = add([own, swap(own, "corpus", bits)], scale, "book_join")
        bits *= 2
    blocks = [own] + [swap(own, "query", k) for k in range(1, query)]
    whole = put(blocks, "query", 1, "book_put")
    grad_codebook = finish(whole, swap(whole, "corpus", 1), "book_finish")
    return grad_queries, grad_codebook, loss


def solution(mesh):
    placed = (P("query", None), P("corpus", None), P("query"), P())
    return jax.shard_map(
        local,
        mesh=mesh,
        in_specs=placed,
        out_specs=(P("query", None), P(), P("query")),
        check_vma=False,
    )
```

```python
import jax
import jax.numpy as jnp
from jax import lax
from jax.experimental import pallas as pl
from jax.experimental.pallas import tpu as pltpu
from jax.sharding import PartitionSpec as P

F32, BF16, I32 = jnp.float32, jnp.bfloat16, jnp.int32
LANES = 128
FINE = 64
VMEM = pl.BlockSpec(memory_space=pltpu.VMEM)
ANY = pl.BlockSpec(memory_space=pl.ANY)
HBM = pl.BlockSpec(memory_space=pltpu.HBM)


def split2(x):
    high = x.astype(BF16)
    return high, (x - high.astype(F32)).astype(BF16)


def split3(x):
    high = x.astype(BF16)
    rest = x - high.astype(F32)
    mid = rest.astype(BF16)
    return high, mid, (rest - mid.astype(F32)).astype(BF16)


def dot(a, b):
    return jnp.dot(a, b, preferred_element_type=F32)


def dot_nt(a, b):
    return lax.dot_general(a, b, (((1,), (1,)), ((), ())), preferred_element_type=F32)


def column(row):
    return jnp.broadcast_to(row, (LANES, row.shape[1])).T


def pick_lanes(table, code):
    inner = code & (LANES - 1)
    value = None
    for w in range(table.shape[1] // LANES):
        part = jnp.take_along_axis(
            table[:, w * LANES : (w + 1) * LANES], inner, axis=1, mode="promise_in_bounds"
        )
        value = part if w == 0 else jnp.where(code >= w * LANES, part, value)
    return value


def score_kernel(
    q_hbm, codes_hbm, book_hbm, pos_hbm,
    q_ref, e_ref, hits_ref, r_ref, stats_ref,
    codes_ref, book_ref, pos_ref, qs_ref, s_ref, low_ref, book_t_ref, sems,
):
    rows, width = q_ref.shape
    subs, docs = codes_ref.shape
    loads = [
        pltpu.make_async_copy(src, dst, sems.at[i])
        for i, (src, dst) in enumerate(
            [(book_hbm, book_ref), (codes_hbm, codes_ref), (q_hbm, q_ref), (pos_hbm, pos_ref)]
        )
    ]
    for load in loads:
        load.start()
    loads[0].wait()
    book_t_ref[...] = book_ref[...].T
    loads[1].wait()
    loads[2].wait()
    loads[3].wait()
    high, mid, low = split3(q_ref[...])
    qs_ref[:, 0:width] = low
    qs_ref[:, width : 2 * width] = mid
    qs_ref[:, 2 * width : 3 * width] = high
    tile = 256
    for t in range(docs // tile):
        for sub in range(0, subs, 2):
            for d in range(t * tile, (t + 1) * tile, LANES):
                lanes = slice(d, d + LANES)
                halves = [
                    pick_lanes(
                        book_t_ref[8 * s : 8 * s + 8, :],
                        jnp.broadcast_to(codes_ref[s : s + 1, lanes], (8, LANES)),
                    )
                    for s in (sub, sub + 1)
                ]
                high, mid, low = split3(jnp.concatenate(halves, axis=0))
                r_ref[8 * sub : 8 * sub + 16, lanes] = high
                r_ref[width + 8 * sub : width + 8 * sub + 16, lanes] = mid
                low_ref[8 * sub : 8 * sub + 16, lanes] = low
        lanes = slice(t * tile, (t + 1) * tile)
        small = dot(qs_ref[:, 0 : 2 * width], r_ref[:, lanes]) + dot(
            qs_ref[:, 2 * width :], low_ref[:, lanes]
        )
        middle = dot(qs_ref[:, width:], r_ref[:, lanes])
        s_ref[:, lanes] = (small + middle) + dot(qs_ref[:, 2 * width :], r_ref[0:width, lanes])
    s = s_ref[...]
    top = jnp.max(s, axis=1, keepdims=True)
    e = jnp.exp(s - top)
    e_ref[...] = e
    total = jnp.sum(e, axis=1, keepdims=True)
    wanted = column(pos_ref[...].reshape(1, rows) - lax.axis_index("corpus") * docs)[:, 0:1]
    hits = wanted == lax.broadcasted_iota(I32, s.shape, 1)
    hits_ref[...] = jnp.where(hits, 1.0, 0.0).astype(BF16)
    own = jnp.sum(jnp.where(hits, s, 0.0), axis=1, keepdims=True)
    lane = lax.broadcasted_iota(I32, (rows, LANES), 1)
    packed = jnp.where(lane == 0, top, jnp.where(lane == 1, total, jnp.where(lane == 2, own, 0.0)))
    stats_ref[...] = packed.T[0:8, :]


def spread_kernel(e_ref, r_ref, u_ref):
    width = u_ref.shape[1]
    eh, em = split2(e_ref[...])
    rh, rm = r_ref[0:width, :], r_ref[width:, :]
    u_ref[...] = (dot_nt(em, rh) + dot_nt(eh, rm)) + dot_nt(eh, rh)


def positive_kernel(hits_ref, r_ref, after_ref, p_ref):
    width = p_ref.shape[1]
    hits = hits_ref[...]
    p_ref[...] = dot_nt(hits, r_ref[width:, :]) + dot_nt(hits, r_ref[0:width, :])


def turn_kernel(q_ref, qt_ref):
    rows = q_ref.shape[0]
    high, mid = split2(q_ref[...].T)
    qt_ref[:, 0:rows] = mid
    qt_ref[:, rows : 2 * rows] = high


def join(a, b):
    top = jnp.maximum(a[0:1], b[0:1])
    total = a[1:2] * jnp.exp(a[0:1] - top) + b[1:2] * jnp.exp(b[0:1] - top)
    return top, total, a[2:3] + b[2:3]


def join_kernel(a_ref, b_ref, after_ref, out_ref):
    top, total, own = join(a_ref[...], b_ref[...])
    out_ref[0:1, :] = top
    out_ref[1:2, :] = total
    out_ref[2:3, :] = own


def terms_kernel(a_ref, b_ref, first_ref, u_ref, p_ref, keep_ref, send_ref, loss_ref, scale_ref, scale_col):
    top, total, own = join(a_ref[...], b_ref[...])
    log_total = top + jnp.log(total)
    loss_ref[...] = (log_total - own).reshape(loss_ref.shape)
    scale = jnp.exp(first_ref[0:1, :] - log_total)
    scale_ref[...] = scale
    half = keep_ref.shape[0]
    scale_col[...] = column(scale).reshape(2, half, LANES)
    core = lax.axis_index("corpus") % 2
    keep_ref[...] = u_ref[core] * scale_col[core][:, 0:1] - p_ref[core]
    send_ref[...] = u_ref[1 - core] * scale_col[1 - core][:, 0:1] - p_ref[1 - core]


def book_kernel(
    e_ref, hits_ref, scale_ref, qt_ref, codes_ref,
    keep_ref, send_ref, ws_ref, dg_ref, gt_ref, both_ref,
):
    rows, docs = e_ref.shape
    width, words = gt_ref.shape
    subs = codes_ref.shape[0]
    w = e_ref[...] * column(scale_ref[...])[:, 0:1] - hits_ref[...].astype(F32)
    wh, wm = split2(w)
    ws_ref[0:rows, :] = wh
    ws_ref[rows:, :] = wm
    dg_ref[...] = dot(qt_ref[...], ws_ref[...]) + dot(qt_ref[:, rows:], ws_ref[0:rows, :])
    coarse = words // FINE
    ramp = lax.broadcasted_iota(I32, (FINE, docs), 0).astype(F32).astype(BF16)
    for first in range(0, subs, 4):
        lhs, rhs = [], []
        for sub in range(first, first + 4):
            code = codes_ref[sub : sub + 1, :]
            value = dg_ref[8 * sub : 8 * sub + 8, :]
            high = value.astype(BF16).astype(F32)
            both = jnp.concatenate([high, value - high], axis=0).astype(BF16)
            outer = jnp.broadcast_to((code // FINE).astype(F32), (16, docs)).astype(BF16)
            lhs += [jnp.where(outer == jnp.bfloat16(b), both, jnp.zeros_like(both)) for b in range(coarse)]
            inner = jnp.broadcast_to((code & (FINE - 1)).astype(F32), (16, docs)).astype(BF16)
            inner = jnp.concatenate([inner] * (FINE // 16), axis=0)
            rhs.append(jnp.where(inner == ramp, jnp.ones_like(ramp), jnp.zeros_like(ramp)))
        out = dot_nt(jnp.concatenate(lhs, axis=0), jnp.concatenate(rhs, axis=0))
        for s in range(4):
            mine = out[16 * coarse * s : 16 * coarse * (s + 1), s * FINE : (s + 1) * FINE]
            parts = [mine[16 * b : 16 * b + 8, :] + mine[16 * b + 8 : 16 * b + 16, :] for b in range(coarse)]
            sub = first + s
            gt_ref[8 * sub : 8 * sub + 8, :] = jnp.concatenate(parts, axis=1)
    both_ref[...] = gt_ref[...].T.reshape(both_ref.shape)
    core = lax.axis_index("corpus") % 2
    keep_ref[...] = both_ref[core]
    send_ref[...] = both_ref[1 - core]


def call(kernel, outs, ins, scratch=(), flops=0, mib=16, name=None):
    return pl.pallas_call(
        kernel,
        out_shape=tuple(jax.ShapeDtypeStruct(shape, kind) for shape, kind in outs),
        in_specs=ins,
        out_specs=tuple(VMEM for _ in outs),
        scratch_shapes=list(scratch),
        compiler_params=pltpu.CompilerParams(vmem_limit_bytes=mib * 2**20),
        cost_estimate=pl.CostEstimate(flops=flops, bytes_accessed=2**17, transcendentals=0),
        name=name or kernel.__name__,
    )


def swap(x, axis, bits):
    return lax.ppermute(x, axis, [(i, i ^ bits) for i in range(lax.axis_size(axis))])


def place_of(axis, unit):
    return lax.axis_index(axis) // unit


def cut(keep, got, axis, unit, count, after, name):
    rows, width = keep.shape
    shape = (count, rows // count, width)

    def kernel(keep_ref, got_ref, after_ref, *outs):
        place = place_of(axis, unit)
        for k, out in enumerate(outs):
            out[...] = keep_ref[place ^ k] + got_ref[place ^ k]

    blocks = call(kernel, [(shape[1:], F32)] * count, [VMEM, VMEM, VMEM], mib=4, name=name)(
        keep.reshape(shape), got.reshape(shape), after
    )
    return list(blocks)


def add(pieces, after, name):
    count = len(pieces)

    def kernel(*refs):
        total = refs[0][...]
        for ref in refs[1:count]:
            total = total + ref[...]
        refs[-1][...] = total

    return call(kernel, [(pieces[0].shape, F32)], [VMEM] * (count + len(after)), mib=4, name=name)(
        *pieces, *after
    )[0]


def bit_at(step, core, count):
    return (step + core * (count // 2)) % count


def chip_swap(x, step):
    corpus = lax.axis_size("corpus")
    count = (corpus // 2).bit_length() - 1
    return lax.ppermute(x, "corpus", [(i, i ^ (2 << bit_at(step, i % 2, count))) for i in range(corpus)])


def my_half(step):
    count = (lax.axis_size("corpus") // 2).bit_length() - 1
    me = lax.axis_index("corpus")
    return (me >> (1 + bit_at(step, me % 2, count))) & 1


def halve(keep, got, step, after, name):
    rows, width = keep.shape
    shape = (2, rows // 2, width)

    def kernel(keep_ref, got_ref, *refs):
        mine = my_half(step)
        refs[-2][...] = keep_ref[mine] + got_ref[mine]
        refs[-1][...] = keep_ref[1 - mine] + got_ref[1 - mine]

    return call(kernel, [(shape[1:], F32)] * 2, [VMEM] * (2 + len(after)), mib=4, name=name)(
        keep.reshape(shape), got.reshape(shape), *after
    )


def rejoin(own, got, step, after, name):
    rows, width = own.shape

    def kernel(own_ref, got_ref, *refs):
        mine = my_half(step)
        refs[-1][mine] = own_ref[...]
        refs[-1][1 - mine] = got_ref[...]

    whole = call(kernel, [((2, rows, width), F32)], [VMEM] * (2 + len(after)), mib=4, name=name)(own, got, *after)[0]
    return whole.reshape(2 * rows, width)


def put(pieces, axis, unit, after, name):
    rows, width = pieces[0].shape

    count = len(pieces)

    def kernel(*refs):
        place = place_of(axis, unit)
        for k, ref in enumerate(refs[:count]):
            refs[-1][place ^ k] = ref[...]

    whole = call(kernel, [((count, rows, width), F32)], [VMEM] * (count + len(after)), mib=4, name=name)(
        *pieces, *after
    )[0]
    return whole.reshape(count * rows, width)


def finish(own, got, after, name):
    rows, width = own.shape

    def kernel(own_ref, got_ref, *refs):
        out_hbm, token_ref, sems = refs[len(after) :]
        token_ref[...] = own_ref[0:8, 0:LANES]
        core = lax.axis_index("corpus") % 2
        copies = [
            pltpu.make_async_copy(own_ref, out_hbm.at[core], sems.at[0]),
            pltpu.make_async_copy(got_ref, out_hbm.at[1 - core], sems.at[1]),
        ]
        for copy in copies:
            copy.start()
        for copy in copies:
            copy.wait()

    whole, token = pl.pallas_call(
        kernel,
        out_shape=(jax.ShapeDtypeStruct((2, rows, width), F32), jax.ShapeDtypeStruct((8, LANES), F32)),
        in_specs=[VMEM] * (2 + len(after)),
        out_specs=(ANY, VMEM),
        scratch_shapes=[pltpu.SemaphoreType.DMA((2,))],
        compiler_params=pltpu.CompilerParams(vmem_limit_bytes=4 * 2**20),
        name=name,
    )(own, got, *after)
    return whole.reshape(2 * rows, width), token


def local(queries, codes, positive, codebook):
    rows, width = queries.shape
    docs, subs = codes.shape
    words = codebook.shape[0]
    corpus, query = lax.axis_size("corpus"), lax.axis_size("query")
    chips = corpus // 2
    codes_t = codes.T
    work = rows * docs * width
    q, e, hits, r, stats = call(
        score_kernel,
        [((rows, width), F32), ((rows, docs), F32), ((rows, docs), BF16), ((2 * width, docs), BF16), ((8, rows), F32)],
        [HBM] * 4,
        [
            pltpu.VMEM((subs, docs), I32),
            pltpu.VMEM((words, width), F32),
            pltpu.VMEM((rows,), I32),
            pltpu.VMEM((rows, 3 * width), BF16),
            pltpu.VMEM((rows, docs), F32),
            pltpu.VMEM((width, docs), BF16),
            pltpu.VMEM((width, words), F32),
            pltpu.SemaphoreType.DMA((4,)),
        ],
        12 * work,
        24,
    )(*[pltpu.with_memory_space_constraint(x, pltpu.HBM) for x in (queries, codes_t, codebook, positive)])
    u = call(spread_kernel, [((rows, width), F32)], [VMEM] * 2, (), 6 * work)(e, r)[0]
    qt = call(turn_kernel, [((width, 2 * rows), BF16)], [VMEM], (), work)(q)[0]
    joined, got, bits, after = stats, swap(stats, "corpus", 1), 2, qt
    while bits < corpus:
        joined = call(join_kernel, [((8, rows), F32)], [VMEM] * 3, mib=4)(joined, got, after)[0]
        got = swap(joined, "corpus", bits)
        after = u
        bits *= 2
    p = call(positive_kernel, [((rows, width), F32)], [VMEM] * 3, (), 4 * work)(hits, r, joined)[0]
    half = rows // 2
    keep, send, loss, scale = call(
        terms_kernel,
        [((half, width), F32), ((half, width), F32), ((rows,), F32), ((1, rows), F32)],
        [VMEM] * 5,
        [pltpu.VMEM((2, half, LANES), F32)],
        mib=8,
    )(joined, got, stats, u.reshape(2, half, width), p.reshape(2, half, width))

    part_rows = words // 2
    book_keep, book_send = call(
        book_kernel,
        [((part_rows, width), F32)] * 2,
        [VMEM] * 5,
        [
            pltpu.VMEM((2 * rows, docs), BF16),
            pltpu.VMEM((width, docs), F32),
            pltpu.VMEM((width, words), F32),
            pltpu.VMEM((2, part_rows, width), F32),
        ],
        14 * work,
    )(e, hits, scale, qt, codes_t)

    bits = chips.bit_length() - 1
    q_keep, q_send = halve(keep, swap(send, "corpus", 1), 0, [], "query_halve")
    b_cuts = cut(book_keep, swap(book_send, "corpus", 1), "query", 1, query, scale, "book_cut")
    b_got = [swap(b_cuts[k], "query", k) for k in range(1, query)]
    b_own = b_sum = add([b_cuts[0]] + b_got, [], "book_sum")
    for step in range(bits - 1):
        q_got = chip_swap(q_send, step)
        if step < bits - 2:
            q_keep, q_send = halve(q_keep, q_got, step + 1, [], "query_halve")
    q_own = add([q_keep, q_got], [b_sum], "query_add")
    for step in range(bits - 1):
        b_own = add([b_own, chip_swap(b_own, step)], [], "book_join")
    b_mid = b_own
    b_last = chip_swap(b_own, bits - 1)
    q_last = chip_swap(q_own, bits - 1)
    b_own = add([b_own, b_last], [], "book_join")
    q_own = add([q_own, q_last], [b_own], "query_all")
    blocks = [b_own] + [swap(b_own, "query", k) for k in range(1, query)]
    b_whole = put(blocks, "query", 1, [], "book_put")
    q_whole = q_own
    for step in reversed(range(bits - 1)):
        q_whole = rejoin(q_whole, chip_swap(q_whole, step), step, [b_whole], "query_put")
    grad_codebook, token = finish(b_whole, swap(b_whole, "corpus", 1), [], "book_finish")
    grad_queries, token = finish(q_whole, swap(q_whole, "corpus", 1), [token], "query_finish")
    return grad_queries, grad_codebook, loss


def solution(mesh):
    placed = (P("query", None), P("corpus", None), P("query"), P())
    return jax.shard_map(
        local,
        mesh=mesh,
        in_specs=placed,
        out_specs=(P("query", None), P(), P("query")),
        check_vma=False,
    )
```

```python
import jax
import jax.numpy as jnp
from jax import lax
from jax.experimental import pallas as pl
from jax.experimental.pallas import tpu as pltpu
from jax.sharding import PartitionSpec as P

F32, BF16, I32 = jnp.float32, jnp.bfloat16, jnp.int32
LANES = 128
FINE = 64
VMEM = pl.BlockSpec(memory_space=pltpu.VMEM)
ANY = pl.BlockSpec(memory_space=pl.ANY)
HBM = pl.BlockSpec(memory_space=pltpu.HBM)


def split2(x):
    high = x.astype(BF16)
    return high, (x - high.astype(F32)).astype(BF16)


def split3(x):
    high = x.astype(BF16)
    rest = x - high.astype(F32)
    mid = rest.astype(BF16)
    return high, mid, (rest - mid.astype(F32)).astype(BF16)


def dot(a, b):
    return jnp.dot(a, b, preferred_element_type=F32)


def dot_nt(a, b):
    return lax.dot_general(a, b, (((1,), (1,)), ((), ())), preferred_element_type=F32)


def column(row):
    return jnp.broadcast_to(row, (LANES, row.shape[1])).T


def pick_lanes(table, code):
    inner = code & (LANES - 1)
    value = None
    for w in range(table.shape[1] // LANES):
        part = jnp.take_along_axis(
            table[:, w * LANES : (w + 1) * LANES], inner, axis=1, mode="promise_in_bounds"
        )
        value = part if w == 0 else jnp.where(code >= w * LANES, part, value)
    return value


def score_kernel(
    q_hbm, codes_hbm, book_hbm, pos_hbm,
    q_ref, codes_ref, e_ref, hits_ref, r_ref, stats_ref,
    book_ref, pos_ref, qs_ref, s_ref, low_ref, book_t_ref, sems,
):
    rows, width = q_ref.shape
    subs, docs = codes_ref.shape
    loads = [
        pltpu.make_async_copy(src, dst, sems.at[i])
        for i, (src, dst) in enumerate(
            [(book_hbm, book_ref), (codes_hbm, codes_ref), (q_hbm, q_ref), (pos_hbm, pos_ref)]
        )
    ]
    for load in loads:
        load.start()
    loads[0].wait()
    book_t_ref[...] = book_ref[...].T
    loads[1].wait()
    tile = 256
    for t in range(docs // tile):
        for sub in range(0, subs, 2):
            for d in range(t * tile, (t + 1) * tile, LANES):
                lanes = slice(d, d + LANES)
                halves = [
                    pick_lanes(
                        book_t_ref[8 * s : 8 * s + 8, :],
                        jnp.broadcast_to(codes_ref[s : s + 1, lanes], (8, LANES)),
                    )
                    for s in (sub, sub + 1)
                ]
                high, mid, low = split3(jnp.concatenate(halves, axis=0))
                r_ref[8 * sub : 8 * sub + 16, lanes] = high
                r_ref[width + 8 * sub : width + 8 * sub + 16, lanes] = mid
                low_ref[8 * sub : 8 * sub + 16, lanes] = low
        if t == 0:
            loads[2].wait()
            loads[3].wait()
            high, mid, low = split3(q_ref[...])
            qs_ref[:, 0:width] = low
            qs_ref[:, width : 2 * width] = mid
            qs_ref[:, 2 * width : 3 * width] = high
        lanes = slice(t * tile, (t + 1) * tile)
        small = dot(qs_ref[:, 0 : 2 * width], r_ref[:, lanes]) + dot(
            qs_ref[:, 2 * width :], low_ref[:, lanes]
        )
        middle = dot(qs_ref[:, width:], r_ref[:, lanes])
        s_ref[:, lanes] = (small + middle) + dot(qs_ref[:, 2 * width :], r_ref[0:width, lanes])
    s = s_ref[...]
    top = jnp.max(s, axis=1, keepdims=True)
    e = jnp.exp(s - top)
    e_ref[...] = e
    total = jnp.sum(e, axis=1, keepdims=True)
    wanted = column(pos_ref[...].reshape(1, rows) - lax.axis_index("corpus") * docs)[:, 0:1]
    hits = wanted == lax.broadcasted_iota(I32, s.shape, 1)
    hits_ref[...] = jnp.where(hits, 1.0, 0.0).astype(BF16)
    own = jnp.sum(jnp.where(hits, s, 0.0), axis=1, keepdims=True)
    lane = lax.broadcasted_iota(I32, (rows, LANES), 1)
    packed = jnp.where(lane == 0, top, jnp.where(lane == 1, total, jnp.where(lane == 2, own, 0.0)))
    stats_ref[...] = packed.T[0:8, :]


def spread_kernel(e_ref, r_ref, u_ref):
    width = u_ref.shape[1]
    eh, em = split2(e_ref[...])
    rh, rm = r_ref[0:width, :], r_ref[width:, :]
    u_ref[...] = (dot_nt(em, rh) + dot_nt(eh, rm)) + dot_nt(eh, rh)


def positive_kernel(hits_ref, r_ref, after_ref, p_ref):
    width = p_ref.shape[1]
    hits = hits_ref[...]
    p_ref[...] = dot_nt(hits, r_ref[width:, :]) + dot_nt(hits, r_ref[0:width, :])


def turn_kernel(q_ref, qt_ref):
    rows = q_ref.shape[0]
    high, mid = split2(q_ref[...].T)
    qt_ref[:, 0:rows] = mid
    qt_ref[:, rows : 2 * rows] = high


def join(a, b):
    top = jnp.maximum(a[0:1], b[0:1])
    total = a[1:2] * jnp.exp(a[0:1] - top) + b[1:2] * jnp.exp(b[0:1] - top)
    return top, total, a[2:3] + b[2:3]


def join_kernel(a_ref, b_ref, after_ref, out_ref):
    top, total, own = join(a_ref[...], b_ref[...])
    out_ref[0:1, :] = top
    out_ref[1:2, :] = total
    out_ref[2:3, :] = own


def terms_kernel(a_ref, b_ref, first_ref, u_ref, p_ref, keep_ref, send_ref, loss_ref, scale_ref):
    top, total, own = join(a_ref[...], b_ref[...])
    log_total = top + jnp.log(total)
    loss_ref[...] = log_total - own
    scale = jnp.exp(first_ref[0:1, :] - log_total)
    scale_ref[...] = scale
    half = keep_ref.shape[0]
    core = lax.axis_index("corpus") % 2
    first, second = scale[:, :half], scale[:, half:]
    keep_ref[...] = u_ref[core] * column(jnp.where(core == 0, first, second))[:, 0:1] - p_ref[core]
    send_ref[...] = u_ref[1 - core] * column(jnp.where(core == 0, second, first))[:, 0:1] - p_ref[1 - core]


def doc_kernel(e_ref, hits_ref, scale_ref, qt_ref, dg_ref, ws_ref):
    rows = e_ref.shape[0]
    w = e_ref[...] * column(scale_ref[...])[:, 0:1] - hits_ref[...].astype(F32)
    wh, wm = split2(w)
    ws_ref[0:rows, :] = wh
    ws_ref[rows:, :] = wm
    dg_ref[...] = dot(qt_ref[...], ws_ref[...]) + dot(qt_ref[:, rows:], ws_ref[0:rows, :])


def book_kernel(dg_ref, codes_ref, after_ref, keep_ref, *refs):
    sends, (gt_ref, both_ref) = refs[:-2], refs[-2:]
    width, words = gt_ref.shape
    subs, docs = codes_ref.shape
    coarse = words // FINE
    ramp = lax.broadcasted_iota(I32, (FINE, docs), 0).astype(F32).astype(BF16)
    for first in range(0, subs, 4):
        lhs, rhs = [], []
        for sub in range(first, first + 4):
            code = codes_ref[sub : sub + 1, :]
            value = dg_ref[8 * sub : 8 * sub + 8, :]
            high = value.astype(BF16).astype(F32)
            both = jnp.concatenate([high, value - high], axis=0).astype(BF16)
            outer = jnp.broadcast_to((code // FINE).astype(F32), (16, docs)).astype(BF16)
            lhs += [jnp.where(outer == jnp.bfloat16(b), both, jnp.zeros_like(both)) for b in range(coarse)]
            inner = jnp.broadcast_to((code & (FINE - 1)).astype(F32), (16, docs)).astype(BF16)
            inner = jnp.concatenate([inner] * (FINE // 16), axis=0)
            rhs.append(jnp.where(inner == ramp, jnp.ones_like(ramp), jnp.zeros_like(ramp)))
        out = dot_nt(jnp.concatenate(lhs, axis=0), jnp.concatenate(rhs, axis=0))
        for s in range(4):
            mine = out[16 * coarse * s : 16 * coarse * (s + 1), s * FINE : (s + 1) * FINE]
            parts = [mine[16 * b : 16 * b + 8, :] + mine[16 * b + 8 : 16 * b + 16, :] for b in range(coarse)]
            sub = first + s
            gt_ref[8 * sub : 8 * sub + 8, :] = jnp.concatenate(parts, axis=1)
    both_ref[...] = gt_ref[...].T.reshape(both_ref.shape)
    core = lax.axis_index("corpus") % 2
    keep_ref[...] = both_ref[core]
    piece = width // len(sends)
    for i, send_ref in enumerate(sends):
        send_ref[...] = both_ref[1 - core, :, i * piece : (i + 1) * piece]


def call(kernel, outs, ins, scratch=(), flops=0, mib=16, name=None):
    return pl.pallas_call(
        kernel,
        out_shape=tuple(jax.ShapeDtypeStruct(shape, kind) for shape, kind in outs),
        in_specs=ins,
        out_specs=tuple(VMEM for _ in outs),
        scratch_shapes=list(scratch),
        compiler_params=pltpu.CompilerParams(vmem_limit_bytes=mib * 2**20),
        cost_estimate=pl.CostEstimate(flops=flops, bytes_accessed=2**17, transcendentals=0),
        name=name or kernel.__name__,
    )


def swap(x, axis, bits):
    return lax.ppermute(x, axis, [(i, i ^ bits) for i in range(lax.axis_size(axis))])


def place_of(axis, unit):
    return lax.axis_index(axis) // unit


def cut(keep, got, axis, unit, count, name):
    rows, width = keep.shape
    rows //= count

    def kernel(keep_ref, *refs):
        place = place_of(axis, unit)
        first = 0
        for got_ref in refs[: len(got)]:
            lanes = slice(first, first + got_ref.shape[2])
            for k, out in enumerate(refs[len(got) :]):
                out[:, lanes] = keep_ref[place ^ k, :, lanes] + got_ref[place ^ k]
            first = lanes.stop

    return call(kernel, [((rows, width), F32)] * count, [VMEM] * (1 + len(got)), mib=4, name=name)(
        keep.reshape(count, rows, width), *[g.reshape(count, rows, g.shape[1]) for g in got]
    )


def add(whole, arrived, after, name, cuts=0):
    arrived = [x if isinstance(x, list) else [x] for x in arrived]
    flat = [block for x in arrived for block in x]
    rows, width = whole.shape

    def kernel(whole_ref, *refs):
        out, *blocks = refs[len(flat) + len(after) :]
        refs = iter(refs)
        total = whole_ref[...]
        for x in arrived:
            total = total + jnp.concatenate([next(refs)[...] for _ in x], axis=1)
        out[...] = total
        for i, block in enumerate(blocks):
            block[...] = total[:, i * (width // cuts) : (i + 1) * (width // cuts)]

    outs = [((rows, width), F32)] + [((rows, width // max(cuts, 1)), F32)] * cuts
    specs = [VMEM] * (1 + len(flat) + len(after))
    total, *blocks = call(kernel, outs, specs, mib=4, name=name)(whole, *flat, *after)
    return (total, blocks) if cuts else total


def bit_at(step, core, count):
    return (step + core * (count // 2)) % count


def chip_swap(x, step):
    corpus = lax.axis_size("corpus")
    count = (corpus // 2).bit_length() - 1
    return lax.ppermute(x, "corpus", [(i, i ^ (2 << bit_at(step, i % 2, count))) for i in range(corpus)])


def my_half(step):
    count = (lax.axis_size("corpus") // 2).bit_length() - 1
    me = lax.axis_index("corpus")
    return (me >> (1 + bit_at(step, me % 2, count))) & 1


def halve(keep, got, step, after, name):
    rows, width = keep.shape
    shape = (2, rows // 2, width)

    def kernel(keep_ref, got_ref, *refs):
        mine = my_half(step)
        refs[-2][...] = keep_ref[mine] + got_ref[mine]
        refs[-1][...] = keep_ref[1 - mine] + got_ref[1 - mine]

    return call(kernel, [(shape[1:], F32)] * 2, [VMEM] * (2 + len(after)), mib=4, name=name)(
        keep.reshape(shape), got.reshape(shape), *after
    )


def rejoin(own, got, step, after, name):
    rows, width = own.shape
    piece = width // len(got)

    def kernel(own_ref, *refs):
        mine = my_half(step)
        refs[-1][mine] = own_ref[...]
        for i, got_ref in enumerate(refs[: len(got)]):
            refs[-1][1 - mine, :, i * piece : (i + 1) * piece] = got_ref[...]

    specs = [VMEM] * (1 + len(got) + len(after))
    whole = call(kernel, [((2, rows, width), F32)], specs, mib=4, name=name)(own, *got, *after)[0]
    return whole.reshape(2 * rows, width)


def put(pieces, axis, unit, after, name):
    rows, width = pieces[0].shape

    count = len(pieces)

    def kernel(*refs):
        place = place_of(axis, unit)
        for k, ref in enumerate(refs[:count]):
            refs[-1][place ^ k] = ref[...]

    whole = call(kernel, [((count, rows, width), F32)], [VMEM] * (count + len(after)), mib=4, name=name)(
        *pieces, *after
    )[0]
    return whole.reshape(count * rows, width)


def finish(own, got, loss):
    count = len(own)
    shapes = tuple(pltpu.HBM((2,) + x.shape, F32) for x in own)
    rows = loss.shape[1]

    def stores(place, halves, outs, sems):
        return [
            pltpu.make_async_copy(half, out.at[place], sems.at[i])
            for i, (half, out) in enumerate(zip(halves, outs))
        ]

    def run(copies):
        for copy in copies:
            copy.start()
        for copy in copies:
            copy.wait()

    def first(*refs):
        loss_ref, *halves = refs[: count + 1]
        loss_out, *outs = refs[count + 1 : 2 * count + 2]
        line, sems = refs[-2:]
        line[...] = loss_ref[...].reshape(rows)
        run(
            stores(lax.axis_index("corpus") % 2, halves, outs, sems)
            + [pltpu.make_async_copy(line, loss_out, sems.at[count])]
        )

    def second(*refs):
        run(stores(1 - lax.axis_index("corpus") % 2, refs[count : 2 * count], refs[2 * count : 3 * count], refs[-1]))

    params = pltpu.CompilerParams(vmem_limit_bytes=4 * 2**20)
    loss, *half = pl.pallas_call(
        first, out_shape=(pltpu.HBM((rows,), F32),) + shapes, in_specs=[VMEM] * (count + 1),
        out_specs=(HBM,) * (count + 1), compiler_params=params, name="finish_own",
        scratch_shapes=[pltpu.VMEM((rows,), F32), pltpu.SemaphoreType.DMA((count + 1,))],
    )(loss, *own)
    whole = pl.pallas_call(
        second, out_shape=shapes, in_specs=[HBM] * count + [VMEM] * count, out_specs=(HBM,) * count,
        scratch_shapes=[pltpu.SemaphoreType.DMA((count,))], compiler_params=params,
        input_output_aliases={i: i for i in range(count)}, name="finish_got",
    )(*half, *got)
    return [w.reshape(2 * x.shape[0], x.shape[1]) for w, x in zip(whole, own)] + [loss]


def local(queries, codes, positive, codebook):
    rows, width = queries.shape
    docs, subs = codes.shape
    words = codebook.shape[0]
    corpus, query = lax.axis_size("corpus"), lax.axis_size("query")
    chips = corpus // 2
    codes_t = codes.T
    work = rows * docs * width
    q, codes_here, e, hits, r, stats = call(
        score_kernel,
        [((rows, width), F32), ((subs, docs), I32), ((rows, docs), F32), ((rows, docs), BF16), ((2 * width, docs), BF16), ((8, rows), F32)],
        [HBM] * 4,
        [
            pltpu.VMEM((words, width), F32),
            pltpu.VMEM((rows,), I32),
            pltpu.VMEM((rows, 3 * width), BF16),
            pltpu.VMEM((rows, docs), F32),
            pltpu.VMEM((width, docs), BF16),
            pltpu.VMEM((width, words), F32),
            pltpu.SemaphoreType.DMA((4,)),
        ],
        12 * work,
        24,
    )(*[pltpu.with_memory_space_constraint(x, pltpu.HBM) for x in (queries, codes_t, codebook, positive)])
    u = call(spread_kernel, [((rows, width), F32)], [VMEM] * 2, (), 6 * work)(e, r)[0]
    qt = call(turn_kernel, [((width, 2 * rows), BF16)], [VMEM], (), work)(q)[0]
    joined, got, bits, after = stats, swap(stats, "corpus", 1), 2, qt
    while bits < corpus:
        joined = call(join_kernel, [((8, rows), F32)], [VMEM] * 3, mib=4)(joined, got, after)[0]
        got = swap(joined, "corpus", bits)
        after = u
        bits *= 2
    p = call(positive_kernel, [((rows, width), F32)], [VMEM] * 3, (), 4 * work)(hits, r, joined)[0]
    half = rows // 2
    keep, send, loss, scale = call(
        terms_kernel,
        [((half, width), F32), ((half, width), F32), ((1, rows), F32), ((1, rows), F32)],
        [VMEM] * 5,
        mib=8,
    )(joined, got, stats, u.reshape(2, half, width), p.reshape(2, half, width))

    bits = chips.bit_length() - 1
    part_rows = words // 2
    dg = call(
        doc_kernel, [((width, docs), F32)], [VMEM] * 4, [pltpu.VMEM((2 * rows, docs), BF16)], 6 * work
    )(e, hits, scale, qt)[0]
    q_keep, q_send = halve(keep, swap(send, "corpus", 1), 0, [dg], "query_halve")
    book_keep, *book_send = call(
        book_kernel,
        [((part_rows, width), F32)] + [((part_rows, width // 2), F32)] * 2,
        [VMEM] * 3,
        [pltpu.VMEM((width, words), F32), pltpu.VMEM((2, part_rows, width), F32)],
        8 * work,
    )(dg, codes_here, q_keep)

    b_cuts = cut(book_keep, [swap(x, "corpus", 1) for x in book_send], "query", 1, query, "book_cut")
    b_got = [swap(b_cuts[k], "query", k) for k in range(1, query)]
    b_own = b_sum = add(b_cuts[0], b_got, [], "book_sum")
    for step in range(bits - 1):
        q_got = chip_swap(q_send, step)
        if step < bits - 2:
            q_keep, q_send = halve(q_keep, q_got, step + 1, [], "query_halve")
    q_own, q_parts = add(q_keep, [q_got], [b_cuts[0]], "query_add", 1)
    for step in range(bits - 1):
        b_own = add(b_own, [chip_swap(b_own, step)], [], "book_join")
    b_mid = b_own
    b_own = b_last = add(b_own, [chip_swap(b_own, bits - 1)], [], "book_join")
    blocks = [b_own] + [swap(b_own, "query", k) for k in range(1, query)]
    b_whole = put(blocks, "query", 1, [], "book_put")
    b_got = swap(b_whole, "corpus", 1)
    q_whole, q_parts = add(q_own, [[chip_swap(x, bits - 1) for x in q_parts]], [b_last], "query_all", 1)
    for step in reversed(range(bits - 1)):
        q_got = [chip_swap(x, step) for x in q_parts]
        q_whole, q_parts = rejoin(q_whole, q_got, step, [b_whole], "query_put"), None
        q_parts = [q_whole]
    q_got = swap(q_whole, "corpus", 1)
    grad_queries, grad_codebook, loss = finish([q_whole, b_whole], [q_got, b_got], loss)
    return grad_queries, grad_codebook, loss


def solution(mesh):
    placed = (P("query", None), P("corpus", None), P("query"), P())
    return jax.shard_map(
        local,
        mesh=mesh,
        in_specs=placed,
        out_specs=(P("query", None), P(), P("query")),
        check_vma=False,
    )
```

```python
import jax
import jax.numpy as jnp
from jax import lax
from jax.experimental import pallas as pl
from jax.experimental.pallas import tpu as pltpu
from jax.sharding import PartitionSpec as P

F32, BF16, I32 = jnp.float32, jnp.bfloat16, jnp.int32
LANES = 128
FINE = 64
VMEM = pl.BlockSpec(memory_space=pltpu.VMEM)
ANY = pl.BlockSpec(memory_space=pl.ANY)
HBM = pl.BlockSpec(memory_space=pltpu.HBM)


def split2(x):
    high = x.astype(BF16)
    return high, (x - high.astype(F32)).astype(BF16)


def split3(x):
    high = x.astype(BF16)
    rest = x - high.astype(F32)
    mid = rest.astype(BF16)
    return high, mid, (rest - mid.astype(F32)).astype(BF16)


def dot(a, b):
    return jnp.dot(a, b, preferred_element_type=F32)


def dot_nt(a, b):
    return lax.dot_general(a, b, (((1,), (1,)), ((), ())), preferred_element_type=F32)


def column(row):
    return jnp.broadcast_to(row, (LANES, row.shape[1])).T


def pick_lanes(table, code):
    inner = code & (LANES - 1)
    value = None
    for w in range(table.shape[1] // LANES):
        part = jnp.take_along_axis(
            table[:, w * LANES : (w + 1) * LANES], inner, axis=1, mode="promise_in_bounds"
        )
        value = part if w == 0 else jnp.where(code >= w * LANES, part, value)
    return value


def score_kernel(
    q_hbm, codes_hbm, book_hbm, pos_hbm,
    q_ref, codes_ref, e_ref, hits_ref, r_ref, stats_ref,
    book_ref, pos_ref, qs_ref, s_ref, low_ref, book_t_ref, sems,
):
    rows, width = q_ref.shape
    subs, docs = codes_ref.shape
    loads = [
        pltpu.make_async_copy(src, dst, sems.at[i])
        for i, (src, dst) in enumerate(
            [(book_hbm, book_ref), (codes_hbm, codes_ref), (q_hbm, q_ref), (pos_hbm, pos_ref)]
        )
    ]
    for load in loads:
        load.start()
    loads[0].wait()
    book_t_ref[...] = book_ref[...].T
    loads[1].wait()
    tile = 256
    for t in range(docs // tile):
        for sub in range(0, subs, 2):
            for d in range(t * tile, (t + 1) * tile, LANES):
                lanes = slice(d, d + LANES)
                halves = [
                    pick_lanes(
                        book_t_ref[8 * s : 8 * s + 8, :],
                        jnp.broadcast_to(codes_ref[s : s + 1, lanes], (8, LANES)),
                    )
                    for s in (sub, sub + 1)
                ]
                high, mid, low = split3(jnp.concatenate(halves, axis=0))
                r_ref[8 * sub : 8 * sub + 16, lanes] = high
                r_ref[width + 8 * sub : width + 8 * sub + 16, lanes] = mid
                low_ref[8 * sub : 8 * sub + 16, lanes] = low
        if t == 0:
            loads[2].wait()
            loads[3].wait()
            high, mid, low = split3(q_ref[...])
            qs_ref[:, 0:width] = low
            qs_ref[:, width : 2 * width] = mid
            qs_ref[:, 2 * width : 3 * width] = high
        lanes = slice(t * tile, (t + 1) * tile)
        small = dot(qs_ref[:, 0 : 2 * width], r_ref[:, lanes]) + dot(
            qs_ref[:, 2 * width :], low_ref[:, lanes]
        )
        middle = dot(qs_ref[:, width:], r_ref[:, lanes])
        s_ref[:, lanes] = (small + middle) + dot(qs_ref[:, 2 * width :], r_ref[0:width, lanes])
    s = s_ref[...]
    top = jnp.max(s, axis=1, keepdims=True)
    e = jnp.exp(s - top)
    e_ref[...] = e
    total = jnp.sum(e, axis=1, keepdims=True)
    wanted = column(pos_ref[...].reshape(1, rows) - lax.axis_index("corpus") * docs)[:, 0:1]
    hits = wanted == lax.broadcasted_iota(I32, s.shape, 1)
    hits_ref[...] = jnp.where(hits, 1.0, 0.0).astype(BF16)
    own = jnp.sum(jnp.where(hits, s, 0.0), axis=1, keepdims=True)
    lane = lax.broadcasted_iota(I32, (rows, LANES), 1)
    packed = jnp.where(lane == 0, top, jnp.where(lane == 1, total, jnp.where(lane == 2, own, 0.0)))
    stats_ref[...] = packed.T[0:8, :]


def spread_kernel(e_ref, r_ref, u_ref):
    width = u_ref.shape[1]
    eh, em = split2(e_ref[...])
    rh, rm = r_ref[0:width, :], r_ref[width:, :]
    u_ref[...] = (dot_nt(em, rh) + dot_nt(eh, rm)) + dot_nt(eh, rh)


def positive_kernel(hits_ref, r_ref, after_ref, p_ref):
    width = p_ref.shape[1]
    hits = hits_ref[...]
    p_ref[...] = dot_nt(hits, r_ref[width:, :]) + dot_nt(hits, r_ref[0:width, :])


def turn_kernel(q_ref, qt_ref):
    rows = q_ref.shape[0]
    high, mid = split2(q_ref[...].T)
    qt_ref[:, 0:rows] = mid
    qt_ref[:, rows : 2 * rows] = high


def join(a, b):
    top = jnp.maximum(a[0:1], b[0:1])
    total = a[1:2] * jnp.exp(a[0:1] - top) + b[1:2] * jnp.exp(b[0:1] - top)
    return top, total, a[2:3] + b[2:3]


def join_kernel(a_ref, b_ref, after_ref, out_ref):
    top, total, own = join(a_ref[...], b_ref[...])
    out_ref[0:1, :] = top
    out_ref[1:2, :] = total
    out_ref[2:3, :] = own


def terms_kernel(a_ref, b_ref, first_ref, u_ref, p_ref, keep_ref, send_ref, loss_ref, scale_ref):
    top, total, own = join(a_ref[...], b_ref[...])
    log_total = top + jnp.log(total)
    loss_ref[...] = log_total - own
    scale = jnp.exp(first_ref[0:1, :] - log_total)
    scale_ref[...] = scale
    half = keep_ref.shape[0]
    core = lax.axis_index("corpus") % 2
    first, second = scale[:, :half], scale[:, half:]
    keep_ref[...] = u_ref[core] * column(jnp.where(core == 0, first, second))[:, 0:1] - p_ref[core]
    send_ref[...] = u_ref[1 - core] * column(jnp.where(core == 0, second, first))[:, 0:1] - p_ref[1 - core]


def doc_kernel(e_ref, hits_ref, scale_ref, qt_ref, dg_ref, ws_ref):
    rows = e_ref.shape[0]
    w = e_ref[...] * column(scale_ref[...])[:, 0:1] - hits_ref[...].astype(F32)
    wh, wm = split2(w)
    ws_ref[0:rows, :] = wh
    ws_ref[rows:, :] = wm
    dg_ref[...] = dot(qt_ref[...], ws_ref[...]) + dot(qt_ref[:, rows:], ws_ref[0:rows, :])


def book_kernel(dg_ref, codes_ref, after_ref, keep_ref, *refs):
    sends, (gt_ref, both_ref) = refs[:-2], refs[-2:]
    width, words = gt_ref.shape
    subs, docs = codes_ref.shape
    coarse = words // FINE
    ramp = lax.broadcasted_iota(I32, (FINE, docs), 0).astype(F32).astype(BF16)
    for first in range(0, subs, 4):
        lhs, rhs = [], []
        for sub in range(first, first + 4):
            code = codes_ref[sub : sub + 1, :]
            value = dg_ref[8 * sub : 8 * sub + 8, :]
            high = value.astype(BF16).astype(F32)
            both = jnp.concatenate([high, value - high], axis=0).astype(BF16)
            outer = jnp.broadcast_to((code // FINE).astype(F32), (16, docs)).astype(BF16)
            lhs += [jnp.where(outer == jnp.bfloat16(b), both, jnp.zeros_like(both)) for b in range(coarse)]
            inner = jnp.broadcast_to((code & (FINE - 1)).astype(F32), (16, docs)).astype(BF16)
            inner = jnp.concatenate([inner] * (FINE // 16), axis=0)
            rhs.append(jnp.where(inner == ramp, jnp.ones_like(ramp), jnp.zeros_like(ramp)))
        out = dot_nt(jnp.concatenate(lhs, axis=0), jnp.concatenate(rhs, axis=0))
        for s in range(4):
            mine = out[16 * coarse * s : 16 * coarse * (s + 1), s * FINE : (s + 1) * FINE]
            parts = [mine[16 * b : 16 * b + 8, :] + mine[16 * b + 8 : 16 * b + 16, :] for b in range(coarse)]
            sub = first + s
            gt_ref[8 * sub : 8 * sub + 8, :] = jnp.concatenate(parts, axis=1)
    both_ref[...] = gt_ref[...].T.reshape(both_ref.shape)
    core = lax.axis_index("corpus") % 2
    keep_ref[...] = both_ref[core]
    piece = width // len(sends)
    for i, send_ref in enumerate(sends):
        send_ref[...] = both_ref[1 - core, :, i * piece : (i + 1) * piece]


def call(kernel, outs, ins, scratch=(), flops=0, mib=16, name=None):
    return pl.pallas_call(
        kernel,
        out_shape=tuple(jax.ShapeDtypeStruct(shape, kind) for shape, kind in outs),
        in_specs=ins,
        out_specs=tuple(VMEM for _ in outs),
        scratch_shapes=list(scratch),
        compiler_params=pltpu.CompilerParams(vmem_limit_bytes=mib * 2**20),
        cost_estimate=pl.CostEstimate(flops=flops, bytes_accessed=2**17, transcendentals=0),
        name=name or kernel.__name__,
    )


def swap(x, axis, bits):
    return lax.ppermute(x, axis, [(i, i ^ bits) for i in range(lax.axis_size(axis))])


def place_of(axis, unit):
    return lax.axis_index(axis) // unit


def cut(keep, got, axis, unit, count, name):
    rows, width = keep.shape
    rows //= count

    def kernel(keep_ref, *refs):
        place = place_of(axis, unit)
        first = 0
        for got_ref in refs[: len(got)]:
            lanes = slice(first, first + got_ref.shape[2])
            for k, out in enumerate(refs[len(got) :]):
                out[:, lanes] = keep_ref[place ^ k, :, lanes] + got_ref[place ^ k]
            first = lanes.stop

    return call(kernel, [((rows, width), F32)] * count, [VMEM] * (1 + len(got)), mib=4, name=name)(
        keep.reshape(count, rows, width), *[g.reshape(count, rows, g.shape[1]) for g in got]
    )


def add(whole, arrived, after, name, cuts=0):
    arrived = [x if isinstance(x, list) else [x] for x in arrived]
    flat = [block for x in arrived for block in x]
    rows, width = whole.shape

    def kernel(whole_ref, *refs):
        out, *blocks = refs[len(flat) + len(after) :]
        refs = iter(refs)
        total = whole_ref[...]
        for x in arrived:
            total = total + jnp.concatenate([next(refs)[...] for _ in x], axis=1)
        out[...] = total
        for i, block in enumerate(blocks):
            block[...] = total[:, i * (width // cuts) : (i + 1) * (width // cuts)]

    outs = [((rows, width), F32)] + [((rows, width // max(cuts, 1)), F32)] * cuts
    specs = [VMEM] * (1 + len(flat) + len(after))
    total, *blocks = call(kernel, outs, specs, mib=4, name=name)(whole, *flat, *after)
    return (total, blocks) if cuts else total


def bit_at(step, core, count):
    return (step + core * (count // 2)) % count


def chip_swap(x, step):
    corpus = lax.axis_size("corpus")
    count = (corpus // 2).bit_length() - 1
    return lax.ppermute(x, "corpus", [(i, i ^ (2 << bit_at(step, i % 2, count))) for i in range(corpus)])


def my_half(step):
    count = (lax.axis_size("corpus") // 2).bit_length() - 1
    me = lax.axis_index("corpus")
    return (me >> (1 + bit_at(step, me % 2, count))) & 1


def halve(keep, got, step, after, name):
    rows, width = keep.shape
    shape = (2, rows // 2, width)

    def kernel(keep_ref, got_ref, *refs):
        mine = my_half(step)
        refs[-2][...] = keep_ref[mine] + got_ref[mine]
        refs[-1][...] = keep_ref[1 - mine] + got_ref[1 - mine]

    return call(kernel, [(shape[1:], F32)] * 2, [VMEM] * (2 + len(after)), mib=4, name=name)(
        keep.reshape(shape), got.reshape(shape), *after
    )


def rejoin(own, got, step, after, name):
    rows, width = own.shape
    piece = width // len(got)

    def kernel(own_ref, *refs):
        mine = my_half(step)
        refs[-1][mine] = own_ref[...]
        for i, got_ref in enumerate(refs[: len(got)]):
            refs[-1][1 - mine, :, i * piece : (i + 1) * piece] = got_ref[...]

    specs = [VMEM] * (1 + len(got) + len(after))
    whole = call(kernel, [((2, rows, width), F32)], specs, mib=4, name=name)(own, *got, *after)[0]
    return whole.reshape(2 * rows, width)


def put(pieces, axis, unit, after, name):
    rows, width = pieces[0].shape

    count = len(pieces)

    def kernel(*refs):
        place = place_of(axis, unit)
        for k, ref in enumerate(refs[:count]):
            refs[-1][place ^ k] = ref[...]

    whole = call(kernel, [((count, rows, width), F32)], [VMEM] * (count + len(after)), mib=4, name=name)(
        *pieces, *after
    )[0]
    return whole.reshape(count * rows, width)


def finish(own, got, loss):
    count = len(own)
    shapes = tuple(pltpu.HBM((2,) + x.shape, F32) for x in own)
    rows = loss.shape[1]

    def stores(place, halves, outs, sems):
        return [
            pltpu.make_async_copy(half, out.at[place], sems.at[i])
            for i, (half, out) in enumerate(zip(halves, outs))
        ]

    def run(copies):
        for copy in copies:
            copy.start()
        for copy in copies:
            copy.wait()

    def first(*refs):
        loss_ref, *halves = refs[: count + 1]
        loss_out, *outs = refs[count + 1 : 2 * count + 2]
        line, sems = refs[-2:]
        line[...] = loss_ref[...].reshape(rows)
        run(
            stores(lax.axis_index("corpus") % 2, halves, outs, sems)
            + [pltpu.make_async_copy(line, loss_out, sems.at[count])]
        )

    def second(*refs):
        run(stores(1 - lax.axis_index("corpus") % 2, refs[count : 2 * count], refs[2 * count : 3 * count], refs[-1]))

    params = pltpu.CompilerParams(vmem_limit_bytes=4 * 2**20)
    loss, *half = pl.pallas_call(
        first, out_shape=(pltpu.HBM((rows,), F32),) + shapes, in_specs=[VMEM] * (count + 1),
        out_specs=(HBM,) * (count + 1), compiler_params=params, name="finish_own",
        scratch_shapes=[pltpu.VMEM((rows,), F32), pltpu.SemaphoreType.DMA((count + 1,))],
    )(loss, *own)
    whole = pl.pallas_call(
        second, out_shape=shapes, in_specs=[HBM] * count + [VMEM] * count, out_specs=(HBM,) * count,
        scratch_shapes=[pltpu.SemaphoreType.DMA((count,))], compiler_params=params,
        input_output_aliases={i: i for i in range(count)}, name="finish_got",
    )(*half, *got)
    return [w.reshape(2 * x.shape[0], x.shape[1]) for w, x in zip(whole, own)] + [loss]


def local(queries, codes, positive, codebook):
    rows, width = queries.shape
    docs, subs = codes.shape
    words = codebook.shape[0]
    corpus, query = lax.axis_size("corpus"), lax.axis_size("query")
    chips = corpus // 2
    codes_t = codes.T
    work = rows * docs * width
    q, codes_here, e, hits, r, stats = call(
        score_kernel,
        [((rows, width), F32), ((subs, docs), I32), ((rows, docs), F32), ((rows, docs), BF16), ((2 * width, docs), BF16), ((8, rows), F32)],
        [HBM] * 4,
        [
            pltpu.VMEM((words, width), F32),
            pltpu.VMEM((rows,), I32),
            pltpu.VMEM((rows, 3 * width), BF16),
            pltpu.VMEM((rows, docs), F32),
            pltpu.VMEM((width, docs), BF16),
            pltpu.VMEM((width, words), F32),
            pltpu.SemaphoreType.DMA((4,)),
        ],
        12 * work,
        24,
    )(*[pltpu.with_memory_space_constraint(x, pltpu.HBM) for x in (queries, codes_t, codebook, positive)])
    u = call(spread_kernel, [((rows, width), F32)], [VMEM] * 2, (), 6 * work)(e, r)[0]
    qt = call(turn_kernel, [((width, 2 * rows), BF16)], [VMEM], (), work)(q)[0]
    joined, got, bits, after = stats, swap(stats, "corpus", 1), 2, qt
    while bits < corpus:
        joined = call(join_kernel, [((8, rows), F32)], [VMEM] * 3, mib=4)(joined, got, after)[0]
        got = swap(joined, "corpus", bits)
        after = u
        bits *= 2
    p = call(positive_kernel, [((rows, width), F32)], [VMEM] * 3, (), 4 * work)(hits, r, joined)[0]
    half = rows // 2
    keep, send, loss, scale = call(
        terms_kernel,
        [((half, width), F32), ((half, width), F32), ((1, rows), F32), ((1, rows), F32)],
        [VMEM] * 5,
        mib=8,
    )(joined, got, stats, u.reshape(2, half, width), p.reshape(2, half, width))

    bits = chips.bit_length() - 1
    part_rows = words // 2
    dg = call(
        doc_kernel, [((width, docs), F32)], [VMEM] * 4, [pltpu.VMEM((2 * rows, docs), BF16)], 6 * work
    )(e, hits, scale, qt)[0]
    q_keep, q_send = halve(keep, swap(send, "corpus", 1), 0, [dg], "query_halve")
    book_keep, *book_send = call(
        book_kernel,
        [((part_rows, width), F32)] + [((part_rows, width // 2), F32)] * 2,
        [VMEM] * 3,
        [pltpu.VMEM((width, words), F32), pltpu.VMEM((2, part_rows, width), F32)],
        8 * work,
    )(dg, codes_here, q_keep)

    b_cuts = cut(book_keep, [swap(x, "corpus", 1) for x in book_send], "query", 1, query, "book_cut")
    b_got = [swap(b_cuts[k], "query", k) for k in reversed(range(1, query))][::-1]
    b_own = b_sum = add(b_cuts[0], b_got[::-1], [], "book_sum")
    for step in range(bits - 1):
        q_got = chip_swap(q_send, step)
        if step < bits - 2:
            q_keep, q_send = halve(q_keep, q_got, step + 1, [], "query_halve")
    q_own, q_parts = add(q_keep, [q_got], [b_cuts[0]], "query_add", 1)
    for step in range(bits - 1):
        b_own = add(b_own, [chip_swap(b_own, step)], [], "book_join")
    b_mid = b_own
    b_own = b_last = add(b_own, [chip_swap(b_own, bits - 1)], [], "book_join")
    blocks = [b_own] + [swap(b_own, "query", k) for k in range(1, query)]
    b_whole = put(blocks, "query", 1, [], "book_put")
    b_got = swap(b_whole, "corpus", 1)
    q_whole, q_parts = add(q_own, [[chip_swap(x, bits - 1) for x in q_parts]], [b_last], "query_all", 1)
    for step in reversed(range(bits - 1)):
        q_got = [chip_swap(x, step) for x in q_parts]
        q_whole, q_parts = rejoin(q_whole, q_got, step, [b_whole], "query_put"), None
        q_parts = [q_whole]
    q_got = swap(q_whole, "corpus", 1)
    grad_queries, grad_codebook, loss = finish([q_whole, b_whole], [q_got, b_got], loss)
    return grad_queries, grad_codebook, loss


def solution(mesh):
    placed = (P("query", None), P("corpus", None), P("query"), P())
    return jax.shard_map(
        local,
        mesh=mesh,
        in_specs=placed,
        out_specs=(P("query", None), P(), P("query")),
        check_vma=False,
    )
```

```python
import jax
import jax.numpy as jnp
from jax import lax
from jax.experimental import pallas as pl
from jax.experimental.pallas import tpu as pltpu
from jax.sharding import PartitionSpec as P

F32, BF16, I32 = jnp.float32, jnp.bfloat16, jnp.int32
LANES = 128
FINE = 64
VMEM = pl.BlockSpec(memory_space=pltpu.VMEM)
ANY = pl.BlockSpec(memory_space=pl.ANY)
HBM = pl.BlockSpec(memory_space=pltpu.HBM)


def split2(x):
    high = x.astype(BF16)
    return high, (x - high.astype(F32)).astype(BF16)


def split3(x):
    high = x.astype(BF16)
    rest = x - high.astype(F32)
    mid = rest.astype(BF16)
    return high, mid, (rest - mid.astype(F32)).astype(BF16)


def dot(a, b):
    return jnp.dot(a, b, preferred_element_type=F32)


def dot_nt(a, b):
    return lax.dot_general(a, b, (((1,), (1,)), ((), ())), preferred_element_type=F32)


def column(row):
    return jnp.broadcast_to(row, (LANES, row.shape[1])).T


def pick_lanes(table, code):
    inner = code & (LANES - 1)
    value = None
    for w in range(table.shape[1] // LANES):
        part = jnp.take_along_axis(
            table[:, w * LANES : (w + 1) * LANES], inner, axis=1, mode="promise_in_bounds"
        )
        value = part if w == 0 else jnp.where(code >= w * LANES, part, value)
    return value


def score_kernel(
    q_hbm, codes_hbm, book_hbm, pos_hbm,
    q_ref, codes_ref, e_ref, hits_ref, r_ref, stats_ref,
    book_ref, pos_ref, qs_ref, s_ref, low_ref, book_t_ref, sems,
):
    rows, width = q_ref.shape
    subs, docs = codes_ref.shape
    loads = [
        pltpu.make_async_copy(src, dst, sems.at[i])
        for i, (src, dst) in enumerate(
            [(book_hbm, book_ref), (codes_hbm, codes_ref), (q_hbm, q_ref), (pos_hbm, pos_ref)]
        )
    ]
    for load in loads:
        load.start()
    loads[0].wait()
    book_t_ref[...] = book_ref[...].T
    loads[1].wait()
    tile = 256
    for t in range(docs // tile):
        for sub in range(0, subs, 2):
            for d in range(t * tile, (t + 1) * tile, LANES):
                lanes = slice(d, d + LANES)
                halves = [
                    pick_lanes(
                        book_t_ref[8 * s : 8 * s + 8, :],
                        jnp.broadcast_to(codes_ref[s : s + 1, lanes], (8, LANES)),
                    )
                    for s in (sub, sub + 1)
                ]
                high, mid, low = split3(jnp.concatenate(halves, axis=0))
                r_ref[8 * sub : 8 * sub + 16, lanes] = high
                r_ref[width + 8 * sub : width + 8 * sub + 16, lanes] = mid
                low_ref[8 * sub : 8 * sub + 16, lanes] = low
        if t == 0:
            loads[2].wait()
            loads[3].wait()
            high, mid, low = split3(q_ref[...])
            qs_ref[:, 0:width] = low
            qs_ref[:, width : 2 * width] = mid
            qs_ref[:, 2 * width : 3 * width] = high
        lanes = slice(t * tile, (t + 1) * tile)
        small = dot(qs_ref[:, 0 : 2 * width], r_ref[:, lanes]) + dot(
            qs_ref[:, 2 * width :], low_ref[:, lanes]
        )
        middle = dot(qs_ref[:, width:], r_ref[:, lanes])
        s_ref[:, lanes] = (small + middle) + dot(qs_ref[:, 2 * width :], r_ref[0:width, lanes])
    s = s_ref[...]
    top = jnp.max(s, axis=1, keepdims=True)
    e = jnp.exp(s - top)
    e_ref[...] = e
    total = jnp.sum(e, axis=1, keepdims=True)
    wanted = column(pos_ref[...].reshape(1, rows) - lax.axis_index("corpus") * docs)[:, 0:1]
    hits = wanted == lax.broadcasted_iota(I32, s.shape, 1)
    hits_ref[...] = jnp.where(hits, 1.0, 0.0).astype(BF16)
    own = jnp.sum(jnp.where(hits, s, 0.0), axis=1, keepdims=True)
    lane = lax.broadcasted_iota(I32, (rows, LANES), 1)
    packed = jnp.where(lane == 0, top, jnp.where(lane == 1, total, jnp.where(lane == 2, own, 0.0)))
    stats_ref[...] = packed.T[0:8, :]


def spread_kernel(e_ref, hits_ref, r_ref, u_ref, p_ref):
    rows, width = u_ref.shape
    low = split2(e_ref[...])[1]
    both = dot_nt(jnp.concatenate([low, hits_ref[...]], axis=0), r_ref[0:width, :])
    u_ref[...] = both[0:rows]
    p_ref[...] = both[rows:]


def positive_kernel(e_ref, hits_ref, r_ref, u_part_ref, p_part_ref, after_ref, u_ref, p_ref):
    rows, width = p_ref.shape
    high = e_ref[...].astype(BF16)
    both = dot_nt(jnp.concatenate([high, hits_ref[...]], axis=0), r_ref[width:, :])
    u_ref[...] = (u_part_ref[...] + both[0:rows]) + dot_nt(high, r_ref[0:width, :])
    p_ref[...] = p_part_ref[...] + both[rows:]


def turn_kernel(q_ref, qt_ref):
    rows = q_ref.shape[0]
    high, mid = split2(q_ref[...].T)
    qt_ref[:, 0:rows] = mid
    qt_ref[:, rows : 2 * rows] = high


def join(a, b):
    top = jnp.maximum(a[0:1], b[0:1])
    total = a[1:2] * jnp.exp(a[0:1] - top) + b[1:2] * jnp.exp(b[0:1] - top)
    return top, total, a[2:3] + b[2:3]


def join_kernel(a_ref, b_ref, after_ref, out_ref):
    top, total, own = join(a_ref[...], b_ref[...])
    out_ref[0:1, :] = top
    out_ref[1:2, :] = total
    out_ref[2:3, :] = own


def terms_kernel(a_ref, b_ref, first_ref, u_ref, p_ref, keep_ref, send_ref, loss_ref, scale_ref):
    top, total, own = join(a_ref[...], b_ref[...])
    log_total = top + jnp.log(total)
    loss_ref[...] = log_total - own
    scale = jnp.exp(first_ref[0:1, :] - log_total)
    scale_ref[...] = scale
    half = keep_ref.shape[0]
    core = lax.axis_index("corpus") % 2
    first, second = scale[:, :half], scale[:, half:]
    keep_ref[...] = u_ref[core] * column(jnp.where(core == 0, first, second))[:, 0:1] - p_ref[core]
    send_ref[...] = u_ref[1 - core] * column(jnp.where(core == 0, second, first))[:, 0:1] - p_ref[1 - core]


def doc_kernel(e_ref, hits_ref, scale_ref, qt_ref, dg_ref, ws_ref):
    rows = e_ref.shape[0]
    w = e_ref[...] * column(scale_ref[...])[:, 0:1] - hits_ref[...].astype(F32)
    wh, wm = split2(w)
    ws_ref[0:rows, :] = wh
    ws_ref[rows:, :] = wm
    dg_ref[...] = dot(qt_ref[...], ws_ref[...]) + dot(qt_ref[:, rows:], ws_ref[0:rows, :])


def book_kernel(dg_ref, codes_ref, after_ref, keep_ref, *refs):
    sends, (gt_ref, both_ref) = refs[:-2], refs[-2:]
    width, words = gt_ref.shape
    subs, docs = codes_ref.shape
    coarse = words // FINE
    ramp = lax.broadcasted_iota(I32, (FINE, docs), 0).astype(F32).astype(BF16)
    for first in range(0, subs, 4):
        lhs, rhs = [], []
        for sub in range(first, first + 4):
            code = codes_ref[sub : sub + 1, :]
            value = dg_ref[8 * sub : 8 * sub + 8, :]
            high = value.astype(BF16).astype(F32)
            both = jnp.concatenate([high, value - high], axis=0).astype(BF16)
            outer = jnp.broadcast_to((code // FINE).astype(F32), (16, docs)).astype(BF16)
            lhs += [jnp.where(outer == jnp.bfloat16(b), both, jnp.zeros_like(both)) for b in range(coarse)]
            inner = jnp.broadcast_to((code & (FINE - 1)).astype(F32), (16, docs)).astype(BF16)
            inner = jnp.concatenate([inner] * (FINE // 16), axis=0)
            rhs.append(jnp.where(inner == ramp, jnp.ones_like(ramp), jnp.zeros_like(ramp)))
        out = dot_nt(jnp.concatenate(lhs, axis=0), jnp.concatenate(rhs, axis=0))
        for s in range(4):
            mine = out[16 * coarse * s : 16 * coarse * (s + 1), s * FINE : (s + 1) * FINE]
            parts = [mine[16 * b : 16 * b + 8, :] + mine[16 * b + 8 : 16 * b + 16, :] for b in range(coarse)]
            sub = first + s
            gt_ref[8 * sub : 8 * sub + 8, :] = jnp.concatenate(parts, axis=1)
    both_ref[...] = gt_ref[...].T.reshape(both_ref.shape)
    core = lax.axis_index("corpus") % 2
    keep_ref[...] = both_ref[core]
    piece = width // len(sends)
    for i, send_ref in enumerate(sends):
        send_ref[...] = both_ref[1 - core, :, i * piece : (i + 1) * piece]


def call(kernel, outs, ins, scratch=(), flops=0, mib=16, name=None):
    return pl.pallas_call(
        kernel,
        out_shape=tuple(jax.ShapeDtypeStruct(shape, kind) for shape, kind in outs),
        in_specs=ins,
        out_specs=tuple(VMEM for _ in outs),
        scratch_shapes=list(scratch),
        compiler_params=pltpu.CompilerParams(vmem_limit_bytes=mib * 2**20),
        cost_estimate=pl.CostEstimate(flops=flops, bytes_accessed=2**17, transcendentals=0),
        name=name or kernel.__name__,
    )


def swap(x, axis, bits):
    return lax.ppermute(x, axis, [(i, i ^ bits) for i in range(lax.axis_size(axis))])


def place_of(axis, unit):
    return lax.axis_index(axis) // unit


def cut(keep, got, axis, unit, count, name):
    rows, width = keep.shape
    rows //= count

    def kernel(keep_ref, *refs):
        place = place_of(axis, unit)
        first = 0
        for got_ref in refs[: len(got)]:
            lanes = slice(first, first + got_ref.shape[2])
            for k, out in enumerate(refs[len(got) :]):
                out[:, lanes] = keep_ref[place ^ k, :, lanes] + got_ref[place ^ k]
            first = lanes.stop

    return call(kernel, [((rows, width), F32)] * count, [VMEM] * (1 + len(got)), mib=4, name=name)(
        keep.reshape(count, rows, width), *[g.reshape(count, rows, g.shape[1]) for g in got]
    )


def add(whole, arrived, after, name, cuts=0):
    arrived = [x if isinstance(x, list) else [x] for x in arrived]
    flat = [block for x in arrived for block in x]
    rows, width = whole.shape

    def kernel(whole_ref, *refs):
        out, *blocks = refs[len(flat) + len(after) :]
        refs = iter(refs)
        total = whole_ref[...]
        for x in arrived:
            total = total + jnp.concatenate([next(refs)[...] for _ in x], axis=1)
        out[...] = total
        for i, block in enumerate(blocks):
            block[...] = total[:, i * (width // cuts) : (i + 1) * (width // cuts)]

    outs = [((rows, width), F32)] + [((rows, width // max(cuts, 1)), F32)] * cuts
    specs = [VMEM] * (1 + len(flat) + len(after))
    total, *blocks = call(kernel, outs, specs, mib=4, name=name)(whole, *flat, *after)
    return (total, blocks) if cuts else total


def bit_at(step, core, count):
    return (step + core * (count // 2)) % count


def chip_swap(x, step):
    corpus = lax.axis_size("corpus")
    count = (corpus // 2).bit_length() - 1
    return lax.ppermute(x, "corpus", [(i, i ^ (2 << bit_at(step, i % 2, count))) for i in range(corpus)])


def my_half(step):
    count = (lax.axis_size("corpus") // 2).bit_length() - 1
    me = lax.axis_index("corpus")
    return (me >> (1 + bit_at(step, me % 2, count))) & 1


def halve(keep, got, step, after, name):
    rows, width = keep.shape
    shape = (2, rows // 2, width)

    def kernel(keep_ref, got_ref, *refs):
        mine = my_half(step)
        refs[-2][...] = keep_ref[mine] + got_ref[mine]
        refs[-1][...] = keep_ref[1 - mine] + got_ref[1 - mine]

    return call(kernel, [(shape[1:], F32)] * 2, [VMEM] * (2 + len(after)), mib=4, name=name)(
        keep.reshape(shape), got.reshape(shape), *after
    )


def rejoin(own, got, step, after, name):
    rows, width = own.shape
    piece = width // len(got)

    def kernel(own_ref, *refs):
        mine = my_half(step)
        refs[-1][mine] = own_ref[...]
        for i, got_ref in enumerate(refs[: len(got)]):
            refs[-1][1 - mine, :, i * piece : (i + 1) * piece] = got_ref[...]

    specs = [VMEM] * (1 + len(got) + len(after))
    whole = call(kernel, [((2, rows, width), F32)], specs, mib=4, name=name)(own, *got, *after)[0]
    return whole.reshape(2 * rows, width)


def put(pieces, axis, unit, after, name):
    rows, width = pieces[0].shape

    count = len(pieces)

    def kernel(*refs):
        place = place_of(axis, unit)
        for k, ref in enumerate(refs[:count]):
            refs[-1][place ^ k] = ref[...]

    whole = call(kernel, [((count, rows, width), F32)], [VMEM] * (count + len(after)), mib=4, name=name)(
        *pieces, *after
    )[0]
    return whole.reshape(count * rows, width)


def finish(own, got, loss):
    count = len(own)
    shapes = tuple(pltpu.HBM((2,) + x.shape, F32) for x in own)
    rows = loss.shape[1]

    def stores(place, halves, outs, sems):
        return [
            pltpu.make_async_copy(half, out.at[place], sems.at[i])
            for i, (half, out) in enumerate(zip(halves, outs))
        ]

    def run(copies):
        for copy in copies:
            copy.start()
        for copy in copies:
            copy.wait()

    def first(*refs):
        loss_ref, *halves = refs[: count + 1]
        loss_out, *outs = refs[count + 1 : 2 * count + 2]
        line, sems = refs[-2:]
        line[...] = loss_ref[...].reshape(rows)
        run(
            stores(lax.axis_index("corpus") % 2, halves, outs, sems)
            + [pltpu.make_async_copy(line, loss_out, sems.at[count])]
        )

    def second(*refs):
        run(stores(1 - lax.axis_index("corpus") % 2, refs[count : 2 * count], refs[2 * count : 3 * count], refs[-1]))

    params = pltpu.CompilerParams(vmem_limit_bytes=4 * 2**20)
    loss, *half = pl.pallas_call(
        first, out_shape=(pltpu.HBM((rows,), F32),) + shapes, in_specs=[VMEM] * (count + 1),
        out_specs=(HBM,) * (count + 1), compiler_params=params, name="finish_own",
        scratch_shapes=[pltpu.VMEM((rows,), F32), pltpu.SemaphoreType.DMA((count + 1,))],
    )(loss, *own)
    whole = pl.pallas_call(
        second, out_shape=shapes, in_specs=[HBM] * count + [VMEM] * count, out_specs=(HBM,) * count,
        scratch_shapes=[pltpu.SemaphoreType.DMA((count,))], compiler_params=params,
        input_output_aliases={i: i for i in range(count)}, name="finish_got",
    )(*half, *got)
    return [w.reshape(2 * x.shape[0], x.shape[1]) for w, x in zip(whole, own)] + [loss]


def local(queries, codes, positive, codebook):
    rows, width = queries.shape
    docs, subs = codes.shape
    words = codebook.shape[0]
    corpus, query = lax.axis_size("corpus"), lax.axis_size("query")
    chips = corpus // 2
    codes_t = codes.T
    work = rows * docs * width
    q, codes_here, e, hits, r, stats = call(
        score_kernel,
        [((rows, width), F32), ((subs, docs), I32), ((rows, docs), F32), ((rows, docs), BF16), ((2 * width, docs), BF16), ((8, rows), F32)],
        [HBM] * 4,
        [
            pltpu.VMEM((words, width), F32),
            pltpu.VMEM((rows,), I32),
            pltpu.VMEM((rows, 3 * width), BF16),
            pltpu.VMEM((rows, docs), F32),
            pltpu.VMEM((width, docs), BF16),
            pltpu.VMEM((width, words), F32),
            pltpu.SemaphoreType.DMA((4,)),
        ],
        12 * work,
        24,
    )(*[pltpu.with_memory_space_constraint(x, pltpu.HBM) for x in (queries, codes_t, codebook, positive)])
    u, p = call(spread_kernel, [((rows, width), F32)] * 2, [VMEM] * 3, (), 4 * work)(e, hits, r)
    qt = call(turn_kernel, [((width, 2 * rows), BF16)], [VMEM], (), work)(q)[0]
    joined, got, bits, after = stats, swap(stats, "corpus", 1), 2, qt
    while bits < corpus:
        joined = call(join_kernel, [((8, rows), F32)], [VMEM] * 3, mib=4)(joined, got, after)[0]
        got = swap(joined, "corpus", bits)
        after = u
        bits *= 2
    u, p = call(positive_kernel, [((rows, width), F32)] * 2, [VMEM] * 6, (), 6 * work)(e, hits, r, u, p, joined)
    half = rows // 2
    keep, send, loss, scale = call(
        terms_kernel,
        [((half, width), F32), ((half, width), F32), ((1, rows), F32), ((1, rows), F32)],
        [VMEM] * 5,
        mib=8,
    )(joined, got, stats, u.reshape(2, half, width), p.reshape(2, half, width))

    bits = chips.bit_length() - 1
    part_rows = words // 2
    dg = call(
        doc_kernel, [((width, docs), F32)], [VMEM] * 4, [pltpu.VMEM((2 * rows, docs), BF16)], 6 * work
    )(e, hits, scale, qt)[0]
    q_keep, q_send = halve(keep, swap(send, "corpus", 1), 0, [dg], "query_halve")
    book_keep, *book_send = call(
        book_kernel,
        [((part_rows, width), F32)] + [((part_rows, width // 2), F32)] * 2,
        [VMEM] * 3,
        [pltpu.VMEM((width, words), F32), pltpu.VMEM((2, part_rows, width), F32)],
        8 * work,
    )(dg, codes_here, q_keep)

    b_cuts = cut(book_keep, [swap(x, "corpus", 1) for x in book_send], "query", 1, query, "book_cut")
    b_got = [swap(b_cuts[k], "query", k) for k in range(1, query)]
    b_own = b_sum = add(b_cuts[0], b_got, [], "book_sum")
    for step in range(bits - 1):
        q_got = chip_swap(q_send, step)
        if step < bits - 2:
            q_keep, q_send = halve(q_keep, q_got, step + 1, [], "query_halve")
    q_own, q_parts = add(q_keep, [q_got], [b_cuts[0]], "query_add", 1)
    for step in range(bits - 1):
        b_own = add(b_own, [chip_swap(b_own, step)], [], "book_join")
    b_mid = b_own
    b_own = b_last = add(b_own, [chip_swap(b_own, bits - 1)], [], "book_join")
    blocks = [b_own] + [swap(b_own, "query", k) for k in range(1, query)]
    b_whole = put(blocks, "query", 1, [], "book_put")
    b_got = swap(b_whole, "corpus", 1)
    q_whole, q_parts = add(q_own, [[chip_swap(x, bits - 1) for x in q_parts]], [b_last], "query_all", 1)
    for step in reversed(range(bits - 1)):
        q_got = [chip_swap(x, step) for x in q_parts]
        q_whole, q_parts = rejoin(q_whole, q_got, step, [b_whole], "query_put"), None
        q_parts = [q_whole]
    q_got = swap(q_whole, "corpus", 1)
    grad_queries, grad_codebook, loss = finish([q_whole, b_whole], [q_got, b_got], loss)
    return grad_queries, grad_codebook, loss


def solution(mesh):
    placed = (P("query", None), P("corpus", None), P("query"), P())
    return jax.shard_map(
        local,
        mesh=mesh,
        in_specs=placed,
        out_specs=(P("query", None), P(), P("query")),
        check_vma=False,
    )
```
